32 devices in a mesh: row: 4 (over z), col: 8 (over y, x, core).
Axes of the slice: x: 2, y: 2, z: 4, core: 2. Of those that a mesh axis runs over, the one named last changes fastest.
Arguments:
- noise: float32 [2048, 2048], P(('row', 'col')), may hold values from -22 to 22
- data: float32 [8192, 2048], P(('col', 'row')), may hold values from -22 to 22
- times: float32 [2048], P(('row', 'col')), may hold values from 0 to 1
Outputs:
- path: float32 [2048, 2048], P(('row', 'col'))
- velocity: float32 [2048, 2048], P(('row', 'col'))
The draws below stay inside these ranges and needn't reach their ends.
All inputs are finite; a program needn't handle non-finite values.
Results may differ from the reference program's by a relative error of at most 0.0003.
Values sent between devices are 32-bit elements; how exact they have to be, the bound alone decides.
A program may use at most 192 MiB of HBM per device.

```python
import math
import jax
import jax.numpy as jnp
from jax import lax

D = 2048
DATA_BLK = 1024
ITERS = 2
NOISE = 2048
DATA = 8192


def cluster_means(key):
    groups = DATA // DATA_BLK
    means = jnp.clip(jax.random.normal(jax.random.fold_in(key, 7), (groups, D), jnp.float32), -3.0, 3.0)
    return means * 0.3


def scaled_codes(key, columns):
    first_key = jax.random.fold_in(key, 0)
    base = jnp.clip(jax.random.normal(first_key, (columns, D), jnp.float32), -5.5, 5.5)
    return base


def data_codes(key):
    means = cluster_means(key)
    labels = jnp.arange(DATA, dtype=jnp.int32) // DATA_BLK
    picked = jnp.take(means, labels, axis=0)
    return scaled_codes(jax.random.fold_in(key, 23), DATA) + picked


def draw_noise(key, part):
    means = cluster_means(key)
    key = jax.random.fold_in(key, 11)
    groups = DATA // DATA_BLK
    labels = jnp.arange(NOISE, dtype=jnp.int32) % groups
    picked = jnp.take(means, labels, axis=0)
    return (scaled_codes(key, NOISE) + picked).astype(jnp.float32)


def draw_data(key, part):
    return data_codes(key).astype(jnp.float32)


def block_levels(stream_key, shape, shards, least, top_value):
    gain = 1.0
    for axis_at, shards_of in shards:
        draws = jax.random.uniform(jax.random.fold_in(jax.random.fold_in(stream_key, 6), axis_at), (shards_of,), jnp.float32, least / len(shards), top_value / len(shards))
        gain = gain * jnp.repeat(jnp.exp(draws), shape[axis_at] // shards_of).reshape((-1,) + (1,) * (len(shape) - 1 - axis_at))
    return gain


def setup_inputs(seed: int = 0) -> dict:
    splits = jax.random.split(jax.random.key(seed), 4)
    return {
        "noise": draw_noise(jax.random.fold_in(splits[3], 71), 0),
        "data": draw_data(jax.random.fold_in(splits[3], 71), 0),
        "times": jnp.clip(1.0 * jax.random.uniform(splits[2], (NOISE,), jnp.float32) ** block_levels(splits[2], (NOISE,), ((0, 32),), -0.2, 0.2), 0.0, 1.0),
    }


epsilon = 0.05
highest = lax.Precision.HIGHEST


def cost_block(rows, row_norms, cols, col_norms):
    cross = lax.dot_general(rows, cols, (((1,), (1,)), ((), ())), precision=highest)
    return (row_norms[:, None] + col_norms[None, :] - 2.0 * cross) / D


def reference(noise, data, times):
    row_norms = jnp.sum(noise * noise, axis=1)
    col_norms = jnp.sum(data * data, axis=1)
    block_rows = min(512, NOISE)
    block_count = NOISE // block_rows
    row_blocks = noise.reshape(block_count, block_rows, D)
    norm_blocks = row_norms.reshape(block_count, block_rows)
    col_pot = jnp.zeros((DATA,), jnp.float32)
    for step in range(ITERS):
        def row_lse(args):
            scores = (col_pot[None, :] - cost_block(args[0], args[1], data, col_norms)) / epsilon
            peak = jnp.max(scores, axis=1)
            return peak + jnp.log(jnp.sum(jnp.exp(scores - peak[:, None]), axis=1))

        lse_rows = lax.map(row_lse, (row_blocks, norm_blocks)).reshape(NOISE)
        row_pot = epsilon * math.log(DATA) - epsilon * lse_rows
        pot_blocks = row_pot.reshape(block_count, block_rows)

        def col_step(carry, args):
            scores = (args[2][:, None] - cost_block(args[0], args[1], data, col_norms)) / epsilon
            peak = jnp.maximum(carry[0], jnp.max(scores, axis=0))
            total = carry[1] * jnp.exp(carry[0] - peak) + jnp.sum(jnp.exp(scores - peak[None, :]), axis=0)
            return (peak, total), None

        start = (jnp.full((DATA,), -jnp.inf, jnp.float32), jnp.zeros((DATA,), jnp.float32))
        (peaks, totals), _ = lax.scan(col_step, start, (row_blocks, norm_blocks, pot_blocks))
        col_pot = epsilon * math.log(NOISE) - epsilon * (peaks + jnp.log(totals))

    def target_block(args):
        scores = (col_pot[None, :] - cost_block(args[0], args[1], data, col_norms)) / epsilon
        peak = jnp.max(scores, axis=1)
        weights = jnp.exp(scores - peak[:, None])
        denom = jnp.sum(weights, axis=1)
        numer = jnp.dot(weights, data, precision=highest)
        return numer / denom[:, None]

    targets = lax.map(target_block, (row_blocks, norm_blocks)).reshape(NOISE, D)
    path = (1.0 - times)[:, None] * noise + times[:, None] * targets
    velocity = targets - noise
    return path, velocity
```

```python
import functools
import math

import jax
import jax.numpy as jnp
from jax import lax
from jax.experimental import pallas as pl
from jax.experimental.pallas import tpu as pltpu
from jax.sharding import PartitionSpec as P

ITERS = 2
EPS = 0.05
PAIR = 2
CORES = 2
QUAD = PAIR * CORES
PIECES = 4
f32 = jnp.float32
bf16 = jnp.bfloat16
NT = (((1,), (1,)), ((), ()))
NN = (((1,), (0,)), ((), ()))


def split(value):
    high = value.astype(bf16)
    return high, (value - high.astype(f32)).astype(bf16)


def dot3(ah, al, bh, bl, dims):
    mm = functools.partial(lax.dot_general, dimension_numbers=dims, preferred_element_type=f32)
    return mm(ah, bh) + (mm(al, bh) + mm(ah, bl))


def kernel(
    Z, Y, noise_ref, data_ref, out_ref,
    nf, df, nh, nl, dh, dl, rn, cn, score, st, wh, wl, rs, cs, part, yb, ub, db,
    up_s, up_r, dn_s, dn_r, ys, yr, xs, xr, sib, fs, fr, rss, rsr, css, csr,
    ps, pr, us, ur, vs, vr,
):
    nb, D = noise_ref.shape
    md = data_ref.shape[0]
    G = Z * Y
    R, C = G * nb, QUAD * md
    mc = md // PIECES
    total_noise, total_data = R * QUAD, C * G
    z = lax.axis_index("row")
    col = lax.axis_index("col")
    c = lax.rem(col, CORES)
    x = lax.rem(lax.div(col, CORES), PAIR)
    y = lax.div(col, QUAD)
    g = z * Y + y
    q = x * CORES + c

    def dev(z_, y_, x_, c_):
        return (z_, (y_ * PAIR + x_) * CORES + c_)

    def rc(src, dst, send, recv, device):
        return pltpu.make_async_remote_copy(
            src_ref=src, dst_ref=dst, send_sem=send, recv_sem=recv,
            device_id=device, device_id_type=pl.DeviceIdType.MESH,
        )

    def group_dev(g2):
        return dev(lax.div(g2, Y), lax.rem(g2, Y), x, c)

    def quad_dev(q2):
        return dev(z, y, lax.div(q2, CORES), lax.rem(q2, CORES))

    barrier = pltpu.get_barrier_semaphore()
    for r in range(1, G):
        pl.semaphore_signal(barrier, inc=1, device_id=group_dev(lax.rem(g + r, G)),
                            device_id_type=pl.DeviceIdType.MESH)
    for r in range(1, QUAD):
        pl.semaphore_signal(barrier, inc=1, device_id=quad_dev(lax.rem(q + r, QUAD)),
                            device_id_type=pl.DeviceIdType.MESH)
    pl.semaphore_wait(barrier, G - 1 + QUAD - 1)

    x_dev = dev(z, y, 1 - x, c)
    c_dev = dev(z, y, x, 1 - c)
    qx = (1 - x) * CORES + c
    qc = x * CORES + 1 - c
    qxc = (1 - x) * CORES + 1 - c

    def data_send(k):
        rows = pl.ds(k * mc, mc)
        return rc(data_ref.at[rows], df.at[q, rows], xs.at[k], xr.at[k], x_dev)

    def data_recv(k):
        rows = pl.ds(k * mc, mc)
        return rc(data_ref.at[rows], df.at[qx, rows], xs.at[k], xr.at[k], x_dev)

    def data_forward(k):
        rows = pl.ds(k * mc, mc)
        return rc(df.at[qx, rows], df.at[qx, rows], fs.at[k], fr.at[k], c_dev)

    def data_forwarded(k):
        rows = pl.ds(k * mc, mc)
        return rc(df.at[qxc, rows], df.at[qxc, rows], fs.at[k], fr.at[k], c_dev)

    def up_copy(zz, s):
        slot = nf.at[zz * Y + y]
        return rc(slot, slot, up_s.at[s], up_r.at[s], dev(z + 1, y, x, c))

    def dn_copy(zz, s):
        slot = nf.at[zz * Y + y]
        return rc(slot, slot, dn_s.at[s], dn_r.at[s], dev(z - 1, y, x, c))

    def y_copy(zz, r):
        slot = nf.at[zz * Y + y]
        return rc(slot, slot, ys.at[zz, r], yr.at[zz, y], dev(z, lax.rem(y + r, Y), x, c))

    def y_landed(zz, r):
        y2 = lax.rem(y + r, Y)
        slot = nf.at[zz * Y + y2]
        return rc(slot, slot, ys.at[zz, r], yr.at[zz, y2], dev(z, y2, x, c))

    def y_sends(zz):
        for r in range(1, Y):
            y_copy(zz, r).start()

    for k in range(PIECES):
        data_send(k).start()
    sib_copy = rc(data_ref, df.at[q], sib.at[0], sib.at[1], c_dev)
    sib_copy.start()
    nf[g] = noise_ref[...]
    y_sends(z)
    pl.when(z + 1 < Z)(lambda: up_copy(z, 0).start())
    pl.when(z > 0)(lambda: dn_copy(z, 0).start())
    df[q] = data_ref[...]

    def convert(src, slot, base, at, count, high, low, norm):
        step = 16

        def body(i, carry):
            value = src[slot, pl.ds(pl.multiple_of(base + i * step, step), step), :]
            rows = pl.ds(pl.multiple_of(at + i * step, step), step)
            h, l = split(value)
            high[rows, :] = h
            low[rows, :] = l
            norm[rows, :] = jnp.broadcast_to(
                jnp.sum(value * value, axis=1, keepdims=True), (step, 128))
            return carry

        lax.fori_loop(0, count // step, body, 0)

    def convert_noise(slot):
        convert(nf, slot, 0, slot * nb, nb, nh, nl, rn)

    def convert_data(slot, k, count):
        convert(df, slot, k * mc, slot * md + k * mc, count, dh, dl, cn)

    convert_noise(g)
    convert_data(q, 0, md)
    rc(data_ref, df.at[qc], sib.at[0], sib.at[1], c_dev).wait_recv()
    convert_data(qc, 0, md)

    def y_arrivals(zz):
        for r in range(1, Y):
            y_landed(zz, r).wait_recv()
            convert_noise(zz * Y + lax.rem(y + r, Y))

    for s in range(1, Z):
        lo, hi = z - s, z + s

        @pl.when(lo >= 0)
        def _():
            up_copy(lo, s - 1).wait_recv()
            if s < Z - 1:
                pl.when(z + 1 < Z)(lambda: up_copy(lo, s).start())
            y_sends(lo)

        @pl.when(hi < Z)
        def _():
            dn_copy(hi, s - 1).wait_recv()
            if s < Z - 1:
                pl.when(z > 0)(lambda: dn_copy(hi, s).start())
            y_sends(hi)

        if s <= PIECES:
            data_recv(s - 1).wait_recv()
            data_forward(s - 1).start()

        pl.when(lo >= 0)(lambda: convert_noise(lo * Y + y))
        pl.when(hi < Z)(lambda: convert_noise(hi * Y + y))
        if s == 1:
            y_arrivals(z)
        else:
            pl.when(lo + 1 >= 0)(lambda: y_arrivals(lo + 1))
            pl.when(hi - 1 < Z)(lambda: y_arrivals(hi - 1))
        if s <= PIECES:
            convert_data(qx, s - 1, mc)
            data_forwarded(s - 1).wait_recv()
            convert_data(qxc, s - 1, mc)
    for k in range(Z - 1, PIECES):
        data_recv(k).wait_recv()
        data_forward(k).start()
        convert_data(qx, k, mc)
    pl.when(z - Z + 1 >= 0)(lambda: y_arrivals(z - Z + 1))
    pl.when(z + Z - 1 < Z)(lambda: y_arrivals(z + Z - 1))
    for k in range(Z - 1, PIECES):
        data_forwarded(k).wait_recv()
        convert_data(qxc, k, mc)

    wide = cn.shape[0] // QUAD

    def score_body(i, carry):
        rows = pl.ds(pl.multiple_of(i * wide, wide), wide)
        cross = dot3(nh[...], nl[...], dh[rows, :], dl[rows, :], NT)
        norms = cn[rows, :].T[0:1, :]
        for t in range(wide // 128):
            lanes = slice(t * 128, (t + 1) * 128)
            score[i, :, lanes] = (
                2.0 * cross[:, lanes] - rn[...] - norms[:, lanes]) * (1.0 / (D * EPS))
        return carry

    lax.fori_loop(0, QUAD, score_body, 0)

    lane = lax.broadcasted_iota(jnp.int32, (1, 128), 1)
    sub = lax.broadcasted_iota(jnp.int32, (8, 1), 0)
    block = 32

    def row_pass(pot, weights):
        def body(i, carry):
            rows = pl.ds(pl.multiple_of(i * block, block), block)
            vals = [score[j, rows, :] + (0.0 if pot is None else pot[:, j * md:(j + 1) * md])
                    for j in range(QUAD)]
            peak = functools.reduce(jnp.maximum, vals)
            peak = jnp.max(peak, axis=1, keepdims=True)
            exps = [jnp.exp(v - peak) for v in vals]
            total = jnp.sum(functools.reduce(jnp.add, exps), axis=1, keepdims=True)
            st[rows, :] = jnp.where(lane == 0, peak, total)
            if weights:
                for j in range(QUAD):
                    h, l = split(exps[j])
                    wh[rows, j * md:(j + 1) * md] = h
                    wl[rows, j * md:(j + 1) * md] = l
            return carry

        lax.fori_loop(0, R // block, body, 0)

    def row_copy(ex, r, landed=False):
        g2 = lax.rem(g + r, G)
        at = g2 if landed else g
        return rc(rs.at[ex, at], rs.at[ex, at], rss.at[ex, r], rsr.at[ex, at], group_dev(g2))

    def row_exchange(ex):
        rs[ex, g] = st[...].T[0:8, :]
        for r in range(1, G):
            row_copy(ex, r).start()

    def row_combine(ex):
        for r in range(1, G):
            row_copy(ex, r, True).wait_recv()
        peaks = [rs[ex, k][0:1, :] for k in range(G)]
        top = functools.reduce(jnp.maximum, peaks)
        total = sum(rs[ex, k][1:2, :] * jnp.exp(peaks[k] - top) for k in range(G))
        return top, total

    def col_copy(ex, r, landed=False):
        q2 = lax.rem(q + r, QUAD)
        at = q2 if landed else q
        return rc(cs.at[ex, at], cs.at[ex, at], css.at[ex, r], csr.at[ex, at], quad_dev(q2))

    def spread(row):
        return jnp.broadcast_to(row, (128, row.shape[1])).T

    pot = None
    for step in range(ITERS):
        row_pass(pot, False)
        row_exchange(step)
        top, total = row_combine(step)
        st[...] = spread(math.log(total_data) - (top + jnp.log(total)))
        for j in range(QUAD):
            for t in range(md // 128):
                lanes = slice(t * 128, (t + 1) * 128)
                val = score[j, :, lanes] + st[...]
                peak = jnp.max(val, axis=0, keepdims=True)
                total = jnp.sum(jnp.exp(val - peak), axis=0, keepdims=True)
                cs[step, q, :, j * md + t * 128:j * md + (t + 1) * 128] = jnp.where(
                    sub == 0, peak, total)
        for r in range(1, QUAD):
            col_copy(step, r).start()
        for r in range(1, QUAD):
            col_copy(step, r, True).wait_recv()
        peaks = [cs[step, k][0:1, :] for k in range(QUAD)]
        top = functools.reduce(jnp.maximum, peaks)
        total = sum(cs[step, k][1:2, :] * jnp.exp(peaks[k] - top) for k in range(QUAD))
        pot = math.log(total_noise) - (top + jnp.log(total))

    row_pass(pot, True)
    row_exchange(ITERS)
    mine = st[...].T[0:1, :]
    top, total = row_combine(ITERS)
    st[...] = spread(jnp.exp(mine - top) / total)

    def order(i):
        d = Z - 1 - lax.div(i, 2)
        return jnp.where(lax.rem(i, 2) == 0, z + d, z - d)

    def part_copy(zz, r):
        y2 = lax.rem(y + r, Y)
        return rc(part.at[zz, y2], yb.at[zz, y], ps.at[zz, r], pr.at[zz, y], dev(z, y2, x, c))

    def part_landed(zz, r):
        y2 = lax.rem(y + r, Y)
        return rc(part.at[zz, y2], yb.at[zz, y2], ps.at[zz, r], pr.at[zz, y2], dev(z, y2, x, c))

    def up_part(zz):
        return rc(part.at[zz, y], ub.at[zz], us.at[zz], ur.at[zz], dev(z + 1, y, x, c))

    def dn_part(zz):
        return rc(part.at[zz, y], db.at[zz], vs.at[zz], vr.at[zz], dev(z - 1, y, x, c))

    def partial_body(i, carry):
        zz = order(i)

        @pl.when((zz >= 0) & (zz < Z))
        def _():
            rows = pl.ds(pl.multiple_of(zz * (Y * nb), Y * nb), Y * nb)
            ah, al = wh[rows, :], wl[rows, :]
            scale = st[rows, :]
            for n in range(D // 256):
                lanes = slice(n * 256, (n + 1) * 256)
                numer = dot3(ah, al, dh[:, lanes], dl[:, lanes], NN)
                for t in range(2):
                    piece = numer[:, t * 128:(t + 1) * 128] * scale
                    for k in range(Y):
                        part[zz, k, :, n * 256 + t * 128:n * 256 + (t + 1) * 128] = (
                            piece[k * nb:(k + 1) * nb])
            for r in range(1, Y):
                part_copy(zz, r).start()

        return carry

    lax.fori_loop(0, 2 * Z - 1, partial_body, 0)

    def reduce_body(i, carry):
        zz = order(i)

        @pl.when((zz >= 0) & (zz < Z))
        def _():
            for r in range(1, Y):
                part_landed(zz, r).wait_recv()
                part[zz, y] += yb[zz, lax.rem(y + r, Y)]

            @pl.when((zz >= z) & (z > 0))
            def _():
                up_part(zz).wait_recv()
                part[zz, y] += ub[zz]

            @pl.when((zz <= z) & (z + 1 < Z))
            def _():
                dn_part(zz).wait_recv()
                part[zz, y] += db[zz]

            pl.when(zz > z)(lambda: up_part(zz).start())
            pl.when(zz < z)(lambda: dn_part(zz).start())

        return carry

    lax.fori_loop(0, 2 * Z - 1, reduce_body, 0)
    out_ref[...] = part[z, y]

    for k in range(PIECES):
        data_send(k).wait_send()
        data_forward(k).wait_send()
    sib_copy.wait_send()
    for s in range(Z - 1):
        pl.when((z - s >= 0) & (z + 1 < Z))(lambda: up_copy(z - s, s).wait_send())
        pl.when((z + s < Z) & (z > 0))(lambda: dn_copy(z + s, s).wait_send())
    for ex in range(ITERS + 1):
        for r in range(1, G):
            row_copy(ex, r).wait_send()
    for ex in range(ITERS):
        for r in range(1, QUAD):
            col_copy(ex, r).wait_send()
    for zz in range(Z):
        for r in range(1, Y):
            y_copy(zz, r).wait_send()
            part_copy(zz, r).wait_send()
        pl.when(zz > z)(lambda: up_part(zz).wait_send())
        pl.when(zz < z)(lambda: dn_part(zz).wait_send())


def targets_of(Z, Y, noise, data):
    nb, D = noise.shape
    md = data.shape[0]
    G = Z * Y
    R, C = G * nb, QUAD * md
    V, dma = pltpu.VMEM, pltpu.SemaphoreType.DMA
    flops = 2 * 6 * R * C * D
    return pl.pallas_call(
        functools.partial(kernel, Z, Y),
        out_shape=jax.ShapeDtypeStruct((nb, D), f32),
        in_specs=[pl.BlockSpec(memory_space=pltpu.VMEM)] * 2,
        out_specs=pl.BlockSpec(memory_space=pltpu.VMEM),
        scratch_shapes=[
            V((G, nb, D), f32), V((QUAD, md, D), f32),
            V((R, D), bf16), V((R, D), bf16), V((C, D), bf16), V((C, D), bf16),
            V((R, 128), f32), V((C, 128), f32),
            V((QUAD, R, md), f32), V((R, 128), f32),
            V((R, C), bf16), V((R, C), bf16),
            V((ITERS + 1, G, 8, R), f32), V((ITERS, QUAD, 8, C), f32),
            V((Z, Y, nb, D), f32), V((Z, Y, nb, D), f32), V((Z, nb, D), f32), V((Z, nb, D), f32),
            dma((Z,)), dma((Z,)), dma((Z,)), dma((Z,)),
            dma((Z, Y)), dma((Z, Y)),
            dma((PIECES,)), dma((PIECES,)), dma((2,)), dma((PIECES,)), dma((PIECES,)),
            dma((ITERS + 1, G)), dma((ITERS + 1, G)), dma((ITERS, QUAD)), dma((ITERS, QUAD)),
            dma((Z, Y)), dma((Z, Y)), dma((Z,)), dma((Z,)), dma((Z,)), dma((Z,)),
        ],
        compiler_params=pltpu.CompilerParams(
            collective_id=0, has_side_effects=True, vmem_limit_bytes=60 * 1024 * 1024),
        cost_estimate=pl.CostEstimate(
            flops=flops, bytes_accessed=8 * (R + C) * D, transcendentals=5 * R * C),
    )(noise, data)


def per_device(Z, Y, noise, data, times):
    targets = targets_of(Z, Y, noise, data)
    path = (1.0 - times)[:, None] * noise + times[:, None] * targets
    return (path, targets - noise)


def solution(mesh):
    Z, Y = mesh.shape["row"], mesh.shape["col"] // QUAD
    in_specs = (P(("row", "col"), None), P(("col", "row"), None), P(("row", "col")))
    out_specs = (P(("row", "col"), None), P(("row", "col"), None))
    return jax.shard_map(
        functools.partial(per_device, Z, Y), mesh=mesh, in_specs=in_specs, out_specs=out_specs,
        check_vma=False,
    )
```

```python
import functools
import math

import jax
import jax.numpy as jnp
from jax import lax
from jax.experimental import pallas as pl
from jax.experimental.pallas import tpu as pltpu
from jax.sharding import PartitionSpec as P

ITERS = 2
EPS = 0.05
PAIR = 2
CORES = 2
QUAD = PAIR * CORES
PIECES = 4
AHEAD = 2
f32 = jnp.float32
bf16 = jnp.bfloat16
NT = (((1,), (1,)), ((), ()))
NN = (((1,), (0,)), ((), ()))


def split(value):
    high = value.astype(bf16)
    return high, (value - high.astype(f32)).astype(bf16)


def dot3(ah, al, bh, bl, dims):
    mm = functools.partial(lax.dot_general, dimension_numbers=dims, preferred_element_type=f32)
    return mm(ah, bh) + (mm(al, bh) + mm(ah, bl))


def dot3_stacked(both, bh, bl, dims):
    mm = functools.partial(lax.dot_general, dimension_numbers=dims, preferred_element_type=f32)
    n = both.shape[0] // 2
    pair = mm(both, bh)
    return pair[:n] + (pair[n:] + mm(both[:n], bl))


def kernel(
    Z, Y, noise_ref, data_ref, out_ref,
    nf, df, nh, nl, dh, dl, rn, cn, score, st, wh, wl, rs, cs, part, yb, ub, db,
    up_s, up_r, dn_s, dn_r, ys, yr, xs, xr, sib, fs, fr, rss, rsr, css, csr,
    ps, pr, us, ur, vs, vr,
):
    nb, D = noise_ref.shape
    md = data_ref.shape[0]
    G = Z * Y
    R, C = G * nb, QUAD * md
    mc = md // PIECES
    total_noise, total_data = R * QUAD, C * G
    z = lax.axis_index("row")
    col = lax.axis_index("col")
    c = lax.rem(col, CORES)
    x = lax.rem(lax.div(col, CORES), PAIR)
    y = lax.div(col, QUAD)
    g = z * Y + y
    q = x * CORES + c

    def dev(z_, y_, x_, c_):
        return (z_, (y_ * PAIR + x_) * CORES + c_)

    def rc(src, dst, send, recv, device):
        return pltpu.make_async_remote_copy(
            src_ref=src, dst_ref=dst, send_sem=send, recv_sem=recv,
            device_id=device, device_id_type=pl.DeviceIdType.MESH,
        )

    def group_dev(g2):
        return dev(lax.div(g2, Y), lax.rem(g2, Y), x, c)

    def quad_dev(q2):
        return dev(z, y, lax.div(q2, CORES), lax.rem(q2, CORES))

    barrier = pltpu.get_barrier_semaphore()
    for r in range(1, G):
        pl.semaphore_signal(barrier, inc=1, device_id=group_dev(lax.rem(g + r, G)),
                            device_id_type=pl.DeviceIdType.MESH)
    for r in range(1, QUAD):
        pl.semaphore_signal(barrier, inc=1, device_id=quad_dev(lax.rem(q + r, QUAD)),
                            device_id_type=pl.DeviceIdType.MESH)
    pl.semaphore_wait(barrier, G - 1 + QUAD - 1)

    x_dev = dev(z, y, 1 - x, c)
    c_dev = dev(z, y, x, 1 - c)
    qx = (1 - x) * CORES + c
    qc = x * CORES + 1 - c
    qxc = (1 - x) * CORES + 1 - c

    def data_send(k):
        rows = pl.ds(k * mc, mc)
        return rc(data_ref.at[rows], df.at[q, rows], xs.at[k], xr.at[k], x_dev)

    def data_recv(k):
        rows = pl.ds(k * mc, mc)
        return rc(data_ref.at[rows], df.at[qx, rows], xs.at[k], xr.at[k], x_dev)

    def data_forward(k):
        rows = pl.ds(k * mc, mc)
        return rc(df.at[qx, rows], df.at[qx, rows], fs.at[k], fr.at[k], c_dev)

    def data_forwarded(k):
        rows = pl.ds(k * mc, mc)
        return rc(df.at[qxc, rows], df.at[qxc, rows], fs.at[k], fr.at[k], c_dev)

    def up_copy(zz, s):
        slot = nf.at[zz * Y + y]
        return rc(slot, slot, up_s.at[s], up_r.at[s], dev(z + 1, y, x, c))

    def dn_copy(zz, s):
        slot = nf.at[zz * Y + y]
        return rc(slot, slot, dn_s.at[s], dn_r.at[s], dev(z - 1, y, x, c))

    def y_copy(zz, r):
        slot = nf.at[zz * Y + y]
        return rc(slot, slot, ys.at[zz, r], yr.at[zz, y], dev(z, lax.rem(y + r, Y), x, c))

    def y_landed(zz, r):
        y2 = lax.rem(y + r, Y)
        slot = nf.at[zz * Y + y2]
        return rc(slot, slot, ys.at[zz, r], yr.at[zz, y2], dev(z, y2, x, c))

    def y_sends(zz):
        for r in range(1, Y):
            y_copy(zz, r).start()

    for k in range(AHEAD):
        data_send(k).start()
    sib_copy = rc(data_ref, df.at[q], sib.at[0], sib.at[1], c_dev)
    sib_copy.start()
    nf[g] = noise_ref[...]
    y_sends(z)
    pl.when(z + 1 < Z)(lambda: up_copy(z, 0).start())
    pl.when(z > 0)(lambda: dn_copy(z, 0).start())
    df[q] = data_ref[...]

    def convert(src, slot, base, at, count, high, low, norm):
        step = min(32, count)

        def body(i, carry):
            value = src[slot, pl.ds(pl.multiple_of(base + i * step, step), step), :]
            rows = pl.ds(pl.multiple_of(at + i * step, step), step)
            h, l = split(value)
            high[rows, :] = h
            low[rows, :] = l
            norm[rows, :] = jnp.broadcast_to(
                jnp.sum(value * value, axis=1, keepdims=True), (step, 128))
            return carry

        lax.fori_loop(0, count // step, body, 0)

    def convert_noise(slot):
        convert(nf, slot, 0, slot * nb, nb, nh, nl, rn)

    def convert_data(slot, k, count):
        convert(df, slot, k * mc, slot * md + k * mc, count, dh, dl, cn)

    convert_noise(g)
    convert_data(q, 0, md)
    rc(data_ref, df.at[qc], sib.at[0], sib.at[1], c_dev).wait_recv()
    convert_data(qc, 0, md)

    def y_arrivals(zz):
        for r in range(1, Y):
            y_landed(zz, r).wait_recv()
            convert_noise(zz * Y + lax.rem(y + r, Y))

    for s in range(1, Z):
        lo, hi = z - s, z + s

        @pl.when(lo >= 0)
        def _():
            up_copy(lo, s - 1).wait_recv()
            if s < Z - 1:
                pl.when(z + 1 < Z)(lambda: up_copy(lo, s).start())
            y_sends(lo)

        @pl.when(hi < Z)
        def _():
            dn_copy(hi, s - 1).wait_recv()
            if s < Z - 1:
                pl.when(z > 0)(lambda: dn_copy(hi, s).start())
            y_sends(hi)

        if s <= PIECES:
            data_recv(s - 1).wait_recv()
            data_forward(s - 1).start()
            if s - 1 + AHEAD < PIECES:
                data_send(s - 1 + AHEAD).start()

        pl.when(lo >= 0)(lambda: convert_noise(lo * Y + y))
        pl.when(hi < Z)(lambda: convert_noise(hi * Y + y))
        if s == 1:
            y_arrivals(z)
        else:
            pl.when(lo + 1 >= 0)(lambda: y_arrivals(lo + 1))
            pl.when(hi - 1 < Z)(lambda: y_arrivals(hi - 1))
        if s <= PIECES:
            convert_data(qx, s - 1, mc)
            data_forwarded(s - 1).wait_recv()
            convert_data(qxc, s - 1, mc)
    for k in range(Z - 1, PIECES):
        data_recv(k).wait_recv()
        data_forward(k).start()
        if k + AHEAD < PIECES:
            data_send(k + AHEAD).start()
        convert_data(qx, k, mc)
    pl.when(z - Z + 1 >= 0)(lambda: y_arrivals(z - Z + 1))
    pl.when(z + Z - 1 < Z)(lambda: y_arrivals(z + Z - 1))
    for k in range(Z - 1, PIECES):
        data_forwarded(k).wait_recv()
        convert_data(qxc, k, mc)

    wide = cn.shape[0] // QUAD

    def score_body(i, carry):
        rows = pl.ds(pl.multiple_of(i * wide, wide), wide)
        cross = dot3(nh[...], nl[...], dh[rows, :], dl[rows, :], NT)
        norms = cn[rows, :].T[0:1, :]
        for t in range(wide // 128):
            lanes = slice(t * 128, (t + 1) * 128)
            score[i, :, lanes] = (
                2.0 * cross[:, lanes] - rn[...] - norms[:, lanes]) * (1.0 / (D * EPS))
        return carry

    lax.fori_loop(0, QUAD, score_body, 0)

    lane = lax.broadcasted_iota(jnp.int32, (1, 128), 1)
    sub = lax.broadcasted_iota(jnp.int32, (8, 1), 0)
    block = 128

    def row_pass(pot, weights):
        def body(i, carry):
            rows = pl.ds(pl.multiple_of(i * block, block), block)
            vals = [score[j, rows, :] + (0.0 if pot is None else pot[:, j * md:(j + 1) * md])
                    for j in range(QUAD)]
            peak = functools.reduce(jnp.maximum, vals)
            peak = jnp.max(peak, axis=1, keepdims=True)
            exps = [jnp.exp(v - peak) for v in vals]
            total = jnp.sum(functools.reduce(jnp.add, exps), axis=1, keepdims=True)
            st[rows, :] = jnp.where(lane == 0, peak, total)
            if weights:
                for j in range(QUAD):
                    h, l = split(exps[j])
                    wh[rows, j * md:(j + 1) * md] = h
                    wl[rows, j * md:(j + 1) * md] = l
            return carry

        lax.fori_loop(0, R // block, body, 0)

    def row_copy(ex, r, landed=False):
        g2 = lax.rem(g + r, G)
        at = g2 if landed else g
        return rc(rs.at[ex, at], rs.at[ex, at], rss.at[ex, r], rsr.at[ex, at], group_dev(g2))

    def row_exchange(ex):
        rs[ex, g] = st[...].T[0:8, :]
        for r in range(1, G):
            row_copy(ex, r).start()

    def row_combine(ex):
        for r in range(1, G):
            row_copy(ex, r, True).wait_recv()
        peaks = [rs[ex, k][0:1, :] for k in range(G)]
        top = functools.reduce(jnp.maximum, peaks)
        total = sum(rs[ex, k][1:2, :] * jnp.exp(peaks[k] - top) for k in range(G))
        return top, total

    def col_copy(ex, r, landed=False):
        q2 = lax.rem(q + r, QUAD)
        at = q2 if landed else q
        return rc(cs.at[ex, at], cs.at[ex, at], css.at[ex, r], csr.at[ex, at], quad_dev(q2))

    def spread(row):
        return jnp.broadcast_to(row, (128, row.shape[1])).T

    pot = None
    for step in range(ITERS):
        row_pass(pot, False)
        row_exchange(step)
        top, total = row_combine(step)
        st[...] = spread(math.log(total_data) - (top + jnp.log(total)))
        for j in range(QUAD):
            for t in range(md // 128):
                lanes = slice(t * 128, (t + 1) * 128)
                val = score[j, :, lanes] + st[...]
                peak = jnp.max(val, axis=0, keepdims=True)
                total = jnp.sum(jnp.exp(val - peak), axis=0, keepdims=True)
                cs[step, q, :, j * md + t * 128:j * md + (t + 1) * 128] = jnp.where(
                    sub == 0, peak, total)
        for r in range(1, QUAD):
            col_copy(step, r).start()
        for r in range(1, QUAD):
            col_copy(step, r, True).wait_recv()
        peaks = [cs[step, k][0:1, :] for k in range(QUAD)]
        top = functools.reduce(jnp.maximum, peaks)
        total = sum(cs[step, k][1:2, :] * jnp.exp(peaks[k] - top) for k in range(QUAD))
        pot = math.log(total_noise) - (top + jnp.log(total))

    row_pass(pot, True)
    row_exchange(ITERS)
    mine = st[...].T[0:1, :]
    top, total = row_combine(ITERS)
    st[...] = spread(jnp.exp(mine - top) / total)

    far, near = jnp.maximum(z, Z - 1 - z), jnp.minimum(z, Z - 1 - z)
    toward = jnp.where(Z - 1 - z >= z, 1, -1)

    def order(n):
        m = n - (far - near)
        late = near - lax.div(jnp.maximum(m, 0), 2)
        flip = jnp.where(lax.rem(jnp.maximum(m, 0), 2) == 0, 1, -1)
        return z + toward * jnp.where(m < 0, far - n, late * flip)

    def part_copy(zz, r):
        y2 = lax.rem(y + r, Y)
        return rc(part.at[zz, y2], yb.at[zz, y], ps.at[zz, r], pr.at[zz, y], dev(z, y2, x, c))

    def part_landed(zz, r):
        y2 = lax.rem(y + r, Y)
        return rc(part.at[zz, y2], yb.at[zz, y2], ps.at[zz, r], pr.at[zz, y2], dev(z, y2, x, c))

    def up_part(zz):
        return rc(part.at[zz, y], ub.at[zz], us.at[zz], ur.at[zz], dev(z + 1, y, x, c))

    def dn_part(zz):
        return rc(part.at[zz, y], db.at[zz], vs.at[zz], vr.at[zz], dev(z - 1, y, x, c))

    def multiply(zz):
        rows = pl.ds(pl.multiple_of(zz * (Y * nb), Y * nb), Y * nb)
        both = jnp.concatenate([wh[rows, :], wl[rows, :]], axis=0)
        scale = st[rows, :]
        for n in range(D // 256):
            lanes = slice(n * 256, (n + 1) * 256)
            numer = dot3_stacked(both, dh[:, lanes], dl[:, lanes], NN)
            for t in range(2):
                piece = numer[:, t * 128:(t + 1) * 128] * scale
                for k in range(Y):
                    part[zz, k, :, n * 256 + t * 128:n * 256 + (t + 1) * 128] = (
                        piece[k * nb:(k + 1) * nb])

    def reduce_step(zz):
        for r in range(1, Y):
            part[zz, y] += yb[zz, lax.rem(y + r, Y)]

        @pl.when((zz >= z) & (z > 0))
        def _():
            up_part(zz).wait_recv()
            part[zz, y] += ub[zz]

        @pl.when((zz <= z) & (z + 1 < Z))
        def _():
            dn_part(zz).wait_recv()
            part[zz, y] += db[zz]

        pl.when(zz > z)(lambda: up_part(zz).start())
        pl.when(zz < z)(lambda: dn_part(zz).start())

    def reduce_body(n, carry):
        zz, last = order(n), order(n - 1)
        pl.when(n < Z)(lambda: multiply(zz))

        @pl.when(n > 0)
        def _():
            for r in range(1, Y):
                part_copy(last, r).wait_send()
                part_landed(last, r).wait_recv()

        @pl.when(n < Z)
        def _():
            for r in range(1, Y):
                part_copy(zz, r).start()

        pl.when(n > 0)(lambda: reduce_step(last))
        return carry

    lax.fori_loop(0, Z + 1, reduce_body, 0)
    out_ref[...] = part[z, y]

    for k in range(PIECES):
        data_send(k).wait_send()
        data_forward(k).wait_send()
    sib_copy.wait_send()
    for s in range(Z - 1):
        pl.when((z - s >= 0) & (z + 1 < Z))(lambda: up_copy(z - s, s).wait_send())
        pl.when((z + s < Z) & (z > 0))(lambda: dn_copy(z + s, s).wait_send())
    for ex in range(ITERS + 1):
        for r in range(1, G):
            row_copy(ex, r).wait_send()
    for ex in range(ITERS):
        for r in range(1, QUAD):
            col_copy(ex, r).wait_send()
    for zz in range(Z):
        for r in range(1, Y):
            y_copy(zz, r).wait_send()
        pl.when(zz > z)(lambda: up_part(zz).wait_send())
        pl.when(zz < z)(lambda: dn_part(zz).wait_send())


def targets_of(Z, Y, noise, data):
    nb, D = noise.shape
    md = data.shape[0]
    G = Z * Y
    R, C = G * nb, QUAD * md
    V, dma = pltpu.VMEM, pltpu.SemaphoreType.DMA
    flops = 2 * 6 * R * C * D
    return pl.pallas_call(
        functools.partial(kernel, Z, Y),
        out_shape=jax.ShapeDtypeStruct((nb, D), f32),
        in_specs=[pl.BlockSpec(memory_space=pltpu.VMEM)] * 2,
        out_specs=pl.BlockSpec(memory_space=pltpu.VMEM),
        scratch_shapes=[
            V((G, nb, D), f32), V((QUAD, md, D), f32),
            V((R, D), bf16), V((R, D), bf16), V((C, D), bf16), V((C, D), bf16),
            V((R, 128), f32), V((C, 128), f32),
            V((QUAD, R, md), f32), V((R, 128), f32),
            V((R, C), bf16), V((R, C), bf16),
            V((ITERS + 1, G, 8, R), f32), V((ITERS, QUAD, 8, C), f32),
            V((Z, Y, nb, D), f32), V((Z, Y, nb, D), f32), V((Z, nb, D), f32), V((Z, nb, D), f32),
            dma((Z,)), dma((Z,)), dma((Z,)), dma((Z,)),
            dma((Z, Y)), dma((Z, Y)),
            dma((PIECES,)), dma((PIECES,)), dma((2,)), dma((PIECES,)), dma((PIECES,)),
            dma((ITERS + 1, G)), dma((ITERS + 1, G)), dma((ITERS, QUAD)), dma((ITERS, QUAD)),
            dma((Z, Y)), dma((Z, Y)), dma((Z,)), dma((Z,)), dma((Z,)), dma((Z,)),
        ],
        compiler_params=pltpu.CompilerParams(
            collective_id=0, has_side_effects=True, vmem_limit_bytes=60 * 1024 * 1024),
        cost_estimate=pl.CostEstimate(
            flops=flops, bytes_accessed=8 * (R + C) * D, transcendentals=5 * R * C),
    )(noise, data)


def per_device(Z, Y, noise, data, times):
    targets = targets_of(Z, Y, noise, data)
    path = (1.0 - times)[:, None] * noise + times[:, None] * targets
    return (path, targets - noise)


def solution(mesh):
    Z, Y = mesh.shape["row"], mesh.shape["col"] // QUAD
    in_specs = (P(("row", "col"), None), P(("col", "row"), None), P(("row", "col")))
    out_specs = (P(("row", "col"), None), P(("row", "col"), None))
    return jax.shard_map(
        functools.partial(per_device, Z, Y), mesh=mesh, in_specs=in_specs, out_specs=out_specs,
        check_vma=False,
    )
```

```python
import functools
import math

import jax
import jax.numpy as jnp
from jax import lax
from jax.experimental import pallas as pl
from jax.experimental.pallas import tpu as pltpu
from jax.sharding import PartitionSpec as P

ITERS = 2
EPS = 0.05
PAIR = 2
CORES = 2
QUAD = PAIR * CORES
PIECES = 4
HALVES = 2
f32 = jnp.float32
bf16 = jnp.bfloat16
NT = (((1,), (1,)), ((), ()))
NN = (((1,), (0,)), ((), ()))


def split(value):
    high = value.astype(bf16)
    return high, (value - high.astype(f32)).astype(bf16)


def dot3(ah, al, bh, bl, dims):
    mm = functools.partial(lax.dot_general, dimension_numbers=dims, preferred_element_type=f32)
    return mm(ah, bh) + (mm(al, bh) + mm(ah, bl))


def dot3_stacked(both, bh, bl, dims):
    mm = functools.partial(lax.dot_general, dimension_numbers=dims, preferred_element_type=f32)
    n = both.shape[0] // 2
    pair = mm(both, bh)
    return pair[:n] + (pair[n:] + mm(both[:n], bl))


def kernel(
    Z, Y, noise_ref, data_ref, out_ref,
    nf, df, nh, nl, dh, dl, rn, cn, score, st, wh, wl, rs, cs, part, yb, ub, db,
    up_s, up_r, dn_s, dn_r, ys, yr, xs, xr, sib, fs, fr, rss, rsr, css, csr,
    ps, pr, us, ur, vs, vr,
):
    nb, D = noise_ref.shape
    md = data_ref.shape[0]
    G = Z * Y
    R, C = G * nb, QUAD * md
    mc = md // PIECES
    total_noise, total_data = R * QUAD, C * G
    z = lax.axis_index("row")
    col = lax.axis_index("col")
    c = lax.rem(col, CORES)
    x = lax.rem(lax.div(col, CORES), PAIR)
    y = lax.div(col, QUAD)
    g = z * Y + y
    q = x * CORES + c

    def dev(z_, y_, x_, c_):
        return (z_, (y_ * PAIR + x_) * CORES + c_)

    def rc(src, dst, send, recv, device):
        return pltpu.make_async_remote_copy(
            src_ref=src, dst_ref=dst, send_sem=send, recv_sem=recv,
            device_id=device, device_id_type=pl.DeviceIdType.MESH,
        )

    def group_dev(g2):
        return dev(lax.div(g2, Y), lax.rem(g2, Y), x, c)

    def quad_dev(q2):
        return dev(z, y, lax.div(q2, CORES), lax.rem(q2, CORES))

    barrier = pltpu.get_barrier_semaphore()
    for r in range(1, G):
        pl.semaphore_signal(barrier, inc=1, device_id=group_dev(lax.rem(g + r, G)),
                            device_id_type=pl.DeviceIdType.MESH)
    for r in range(1, QUAD):
        pl.semaphore_signal(barrier, inc=1, device_id=quad_dev(lax.rem(q + r, QUAD)),
                            device_id_type=pl.DeviceIdType.MESH)
    pl.semaphore_wait(barrier, G - 1 + QUAD - 1)

    x_dev = dev(z, y, 1 - x, c)
    c_dev = dev(z, y, x, 1 - c)
    qx = (1 - x) * CORES + c
    qc = x * CORES + 1 - c
    qxc = (1 - x) * CORES + 1 - c

    def data_send(k):
        rows = pl.ds(k * mc, mc)
        return rc(data_ref.at[rows], df.at[q, rows], xs.at[k], xr.at[k], x_dev)

    def data_recv(k):
        rows = pl.ds(k * mc, mc)
        return rc(data_ref.at[rows], df.at[qx, rows], xs.at[k], xr.at[k], x_dev)

    def data_forward(k):
        rows = pl.ds(k * mc, mc)
        return rc(df.at[qx, rows], df.at[qx, rows], fs.at[k], fr.at[k], c_dev)

    def data_forwarded(k):
        rows = pl.ds(k * mc, mc)
        return rc(df.at[qxc, rows], df.at[qxc, rows], fs.at[k], fr.at[k], c_dev)

    def up_copy(zz, s):
        slot = nf.at[zz * Y + y]
        return rc(slot, slot, up_s.at[s], up_r.at[s], dev(z + 1, y, x, c))

    def dn_copy(zz, s):
        slot = nf.at[zz * Y + y]
        return rc(slot, slot, dn_s.at[s], dn_r.at[s], dev(z - 1, y, x, c))

    def y_copy(zz, r):
        slot = nf.at[zz * Y + y]
        return rc(slot, slot, ys.at[zz, r], yr.at[zz, y], dev(z, lax.rem(y + r, Y), x, c))

    def y_landed(zz, r):
        y2 = lax.rem(y + r, Y)
        slot = nf.at[zz * Y + y2]
        return rc(slot, slot, ys.at[zz, r], yr.at[zz, y2], dev(z, y2, x, c))

    def y_sends(zz):
        for r in range(1, Y):
            y_copy(zz, r).start()

    for k in range(PIECES - 1):
        data_send(k).start()
    sib_copy = rc(data_ref, df.at[q], sib.at[0], sib.at[1], c_dev)
    sib_copy.start()
    nf[g] = noise_ref[...]
    y_sends(z)
    pl.when(z + 1 < Z)(lambda: up_copy(z, 0).start())
    pl.when(z > 0)(lambda: dn_copy(z, 0).start())
    df[q] = data_ref[...]

    def convert(src, slot, base, at, count, high, low, norm):
        step = min(32, count)

        def body(i, carry):
            value = src[slot, pl.ds(pl.multiple_of(base + i * step, step), step), :]
            rows = pl.ds(pl.multiple_of(at + i * step, step), step)
            h, l = split(value)
            high[rows, :] = h
            low[rows, :] = l
            norm[rows, :] = jnp.broadcast_to(
                jnp.sum(value * value, axis=1, keepdims=True), (step, 128))
            return carry

        lax.fori_loop(0, count // step, body, 0)

    def convert_noise(slot):
        convert(nf, slot, 0, slot * nb, nb, nh, nl, rn)

    def convert_data(slot, k, count):
        convert(df, slot, k * mc, slot * md + k * mc, count, dh, dl, cn)

    convert_noise(g)
    convert_data(q, 0, md)
    rc(data_ref, df.at[qc], sib.at[0], sib.at[1], c_dev).wait_recv()
    convert_data(qc, 0, md)

    def score_block(at, count, j):
        rows, cols = pl.ds(at, count), pl.ds(pl.multiple_of(j * md, md), md)
        both = jnp.concatenate([nh[rows, :], nl[rows, :]], axis=0)
        cross = dot3_stacked(both, dh[cols, :], dl[cols, :], NT)
        norms = cn[cols, :].T[0:1, :]
        for t in range(md // 128):
            lanes = slice(t * 128, (t + 1) * 128)
            score[j, rows, lanes] = (
                2.0 * cross[:, lanes] - rn[rows, :] - norms[:, lanes]) * (1.0 / (D * EPS))

    def y_arrivals(zz):
        for r in range(1, Y):
            y_landed(zz, r).wait_recv()
            convert_noise(zz * Y + lax.rem(y + r, Y))

        def body(i, carry):
            score_block(pl.multiple_of(zz * (Y * nb), Y * nb), Y * nb, x * CORES + i)
            return carry

        lax.fori_loop(0, CORES, body, 0)

    def data_piece(k):
        data_recv(k).wait_recv()
        data_forward(k).start()
        convert_data(qx, k, mc)

    def data_piece_forwarded(k):
        data_forwarded(k).wait_recv()
        convert_data(qxc, k, mc)

    for s in range(1, Z):
        lo, hi = z - s, z + s

        @pl.when(lo >= 0)
        def _():
            up_copy(lo, s - 1).wait_recv()
            if s < Z - 1:
                pl.when(z + 1 < Z)(lambda: up_copy(lo, s).start())
            y_sends(lo)

        @pl.when(hi < Z)
        def _():
            dn_copy(hi, s - 1).wait_recv()
            if s < Z - 1:
                pl.when(z > 0)(lambda: dn_copy(hi, s).start())
            y_sends(hi)

        if s == min(2, Z - 1):
            data_send(PIECES - 1).start()
        pl.when(lo >= 0)(lambda: convert_noise(lo * Y + y))
        pl.when(hi < Z)(lambda: convert_noise(hi * Y + y))
        if s == Z - 1:
            for k in range(PIECES - 1):
                data_piece(k)
            for k in range(PIECES - 1):
                data_piece_forwarded(k)
        if s == 1:
            y_arrivals(z)
        else:
            pl.when(lo + 1 >= 0)(lambda: y_arrivals(lo + 1))
            pl.when(hi - 1 < Z)(lambda: y_arrivals(hi - 1))
    pl.when(z - Z + 1 >= 0)(lambda: y_arrivals(z - Z + 1))
    pl.when(z + Z - 1 < Z)(lambda: y_arrivals(z + Z - 1))
    data_piece(PIECES - 1)
    data_piece_forwarded(PIECES - 1)

    def score_body(i, carry):
        j = (1 - x) * CORES + i
        cols = pl.ds(pl.multiple_of(j * md, md), md)
        cross = dot3(nh[...], nl[...], dh[cols, :], dl[cols, :], NT)
        norms = cn[cols, :].T[0:1, :]
        for t in range(md // 128):
            lanes = slice(t * 128, (t + 1) * 128)
            score[j, :, lanes] = (
                2.0 * cross[:, lanes] - rn[...] - norms[:, lanes]) * (1.0 / (D * EPS))
        return carry

    lax.fori_loop(0, CORES, score_body, 0)

    lane = lax.broadcasted_iota(jnp.int32, (1, 128), 1)
    RB, CB, SB = R // 128, C // 128, md // 128
    block = 128

    def row_pass(pot, weights):
        def shift(j):
            return jnp.concatenate([pot[j * SB + t:j * SB + t + 1] for t in range(SB)], axis=1)

        def body(i, carry):
            rows = pl.ds(pl.multiple_of(i * block, block), block)
            vals = [score[j, rows, :] + (0.0 if pot is None else shift(j))
                    for j in range(QUAD)]
            peak = functools.reduce(jnp.maximum, vals)
            peak = jnp.max(peak, axis=1, keepdims=True)
            exps = [jnp.exp(v - peak) for v in vals]
            total = jnp.sum(functools.reduce(jnp.add, exps), axis=1, keepdims=True)
            st[rows, :] = jnp.where(lane == 0, peak, total)
            if weights:
                for j in range(QUAD):
                    h, l = split(exps[j])
                    wh[rows, j * md:(j + 1) * md] = h
                    wl[rows, j * md:(j + 1) * md] = l
            return carry

        lax.fori_loop(0, R // block, body, 0)

    def row_copy(ex, r, landed=False):
        g2 = lax.rem(g + r, G)
        at = g2 if landed else g
        return rc(rs.at[ex, at], rs.at[ex, at], rss.at[ex, r], rsr.at[ex, at], group_dev(g2))

    def row_exchange(ex):
        for k in range(RB):
            turned = st[k * 128:(k + 1) * 128, :].T
            rs[ex, g, k:k + 1, :] = turned[0:1]
            rs[ex, g, RB + k:RB + k + 1, :] = turned[1:2]
        for r in range(1, G):
            row_copy(ex, r).start()

    def row_combine(ex):
        for r in range(1, G):
            row_copy(ex, r, True).wait_recv()
        peaks = [rs[ex, k, 0:RB, :] for k in range(G)]
        top = functools.reduce(jnp.maximum, peaks)
        total = sum(rs[ex, k, RB:2 * RB, :] * jnp.exp(peaks[k] - top) for k in range(G))
        return top, total

    def col_copy(ex, r, landed=False):
        q2 = lax.rem(q + r, QUAD)
        at = q2 if landed else q
        return rc(cs.at[ex, at], cs.at[ex, at], css.at[ex, r], csr.at[ex, at], quad_dev(q2))

    def spread(packed):
        for k in range(RB):
            st[k * 128:(k + 1) * 128, :] = jnp.broadcast_to(packed[k:k + 1], (128, 128)).T

    pot = None
    for step in range(ITERS):
        row_pass(pot, False)
        row_exchange(step)
        top, total = row_combine(step)
        spread(math.log(total_data) - (top + jnp.log(total)))
        for j in range(QUAD):
            for t in range(SB):
                lanes, at = slice(t * 128, (t + 1) * 128), j * SB + t
                val = score[j, :, lanes] + st[...]
                peak = jnp.max(val, axis=0, keepdims=True)
                total = jnp.sum(jnp.exp(val - peak), axis=0, keepdims=True)
                cs[step, q, at:at + 1, :] = peak
                cs[step, q, CB + at:CB + at + 1, :] = total
        for r in range(1, QUAD):
            col_copy(step, r).start()
        for r in range(1, QUAD):
            col_copy(step, r, True).wait_recv()
        peaks = [cs[step, k, 0:CB, :] for k in range(QUAD)]
        top = functools.reduce(jnp.maximum, peaks)
        total = sum(cs[step, k, CB:2 * CB, :] * jnp.exp(peaks[k] - top) for k in range(QUAD))
        pot = math.log(total_noise) - (top + jnp.log(total))

    row_pass(pot, True)
    row_exchange(ITERS)
    far, near = jnp.maximum(z, Z - 1 - z), jnp.minimum(z, Z - 1 - z)
    toward = jnp.where(Z - 1 - z >= z, 1, -1)

    def order(n):
        m = n - (far - near)
        late = near - lax.div(jnp.maximum(m, 0), 2)
        flip = jnp.where(lax.rem(jnp.maximum(m, 0), 2) == 0, 1, -1)
        return z + toward * jnp.where(m < 0, far - n, late * flip)

    half = nb // HALVES

    def part_copy(zz, h, r, landed=False):
        y2 = lax.rem(y + r, Y)
        rows, at = pl.ds(pl.multiple_of(h * half, half), half), y2 if landed else y
        return rc(part.at[zz, y2, rows], yb.at[zz, at, rows],
                  ps.at[zz, h, r], pr.at[zz, h, at], dev(z, y2, x, c))

    def up_part(zz, h):
        rows = pl.ds(pl.multiple_of(h * half, half), half)
        return rc(part.at[zz, y, rows], ub.at[zz, rows], us.at[zz, h], ur.at[zz, h],
                  dev(z + 1, y, x, c))

    def dn_part(zz, h):
        rows = pl.ds(pl.multiple_of(h * half, half), half)
        return rc(part.at[zz, y, rows], db.at[zz, rows], vs.at[zz, h], vr.at[zz, h],
                  dev(z - 1, y, x, c))

    def multiply(zz, scaled):
        rows = pl.ds(pl.multiple_of(zz * (Y * nb), Y * nb), Y * nb)
        both = jnp.concatenate([wh[rows, :], wl[rows, :]], axis=0)
        for n in range(D // 256):
            lanes = slice(n * 256, (n + 1) * 256)
            numer = dot3_stacked(both, dh[:, lanes], dl[:, lanes], NN)
            for t in range(2):
                piece = numer[:, t * 128:(t + 1) * 128]
                if scaled:
                    piece = piece * st[rows, :]
                for k in range(Y):
                    part[zz, k, :, n * 256 + t * 128:n * 256 + (t + 1) * 128] = (
                        piece[k * nb:(k + 1) * nb])

    def part_sends(p):
        for r in range(1, Y):
            part_copy(order(lax.div(p, HALVES)), lax.rem(p, HALVES), r).start()

    first = order(jnp.int32(0))
    multiply(first, False)
    top, total = row_combine(ITERS)
    spread(jnp.exp(rs[ITERS, g, 0:RB, :] - top) / total)
    for k in range(Y):
        scale = st[pl.ds(pl.multiple_of(first * (Y * nb), Y * nb) + k * nb, nb), :]
        for t in range(D // 128):
            part[first, k, :, t * 128:(t + 1) * 128] *= scale
    for p in range(HALVES):
        part_sends(jnp.int32(p))

    def multiply_body(n, carry):
        multiply(order(n), True)
        return carry

    lax.fori_loop(1, Z, multiply_body, 0)

    def reduce_body(p, carry):
        zz, h = order(lax.div(p, HALVES)), lax.rem(p, HALVES)
        rows = pl.ds(pl.multiple_of(h * half, half), half)
        for r in range(1, Y):
            part_copy(zz, h, r, True).wait_recv()
        pl.when(p + HALVES < Z * HALVES)(lambda: part_sends(p + HALVES))
        for r in range(1, Y):
            part[zz, y, rows, :] += yb[zz, lax.rem(y + r, Y), rows, :]

        @pl.when((zz >= z) & (z > 0))
        def _():
            up_part(zz, h).wait_recv()
            part[zz, y, rows, :] += ub[zz, rows, :]

        @pl.when((zz <= z) & (z + 1 < Z))
        def _():
            dn_part(zz, h).wait_recv()
            part[zz, y, rows, :] += db[zz, rows, :]

        pl.when(zz > z)(lambda: up_part(zz, h).start())
        pl.when(zz < z)(lambda: dn_part(zz, h).start())
        return carry

    lax.fori_loop(0, Z * HALVES, reduce_body, 0)
    out_ref[...] = part[z, y]

    for k in range(PIECES):
        data_send(k).wait_send()
        data_forward(k).wait_send()
    sib_copy.wait_send()
    for s in range(Z - 1):
        pl.when((z - s >= 0) & (z + 1 < Z))(lambda: up_copy(z - s, s).wait_send())
        pl.when((z + s < Z) & (z > 0))(lambda: dn_copy(z + s, s).wait_send())
    for ex in range(ITERS + 1):
        for r in range(1, G):
            row_copy(ex, r).wait_send()
    for ex in range(ITERS):
        for r in range(1, QUAD):
            col_copy(ex, r).wait_send()
    for zz in range(Z):
        for r in range(1, Y):
            y_copy(zz, r).wait_send()
        for h in range(HALVES):
            for r in range(1, Y):
                part_copy(zz, h, r).wait_send()
            pl.when(zz > z)(lambda: up_part(zz, h).wait_send())
            pl.when(zz < z)(lambda: dn_part(zz, h).wait_send())


def targets_of(Z, Y, noise, data):
    nb, D = noise.shape
    md = data.shape[0]
    G = Z * Y
    R, C = G * nb, QUAD * md
    V, dma = pltpu.VMEM, pltpu.SemaphoreType.DMA
    flops = 2 * 6 * R * C * D
    return pl.pallas_call(
        functools.partial(kernel, Z, Y),
        out_shape=jax.ShapeDtypeStruct((nb, D), f32),
        in_specs=[pl.BlockSpec(memory_space=pltpu.VMEM)] * 2,
        out_specs=pl.BlockSpec(memory_space=pltpu.VMEM),
        scratch_shapes=[
            V((G, nb, D), f32), V((QUAD, md, D), f32),
            V((R, D), bf16), V((R, D), bf16), V((C, D), bf16), V((C, D), bf16),
            V((R, 128), f32), V((C, 128), f32),
            V((QUAD, R, md), f32), V((R, 128), f32),
            V((R, C), bf16), V((R, C), bf16),
            V((ITERS + 1, G, R // 64, 128), f32), V((ITERS, QUAD, C // 64, 128), f32),
            V((Z, Y, nb, D), f32), V((Z, Y, nb, D), f32), V((Z, nb, D), f32), V((Z, nb, D), f32),
            dma((Z,)), dma((Z,)), dma((Z,)), dma((Z,)),
            dma((Z, Y)), dma((Z, Y)),
            dma((PIECES,)), dma((PIECES,)), dma((2,)), dma((PIECES,)), dma((PIECES,)),
            dma((ITERS + 1, G)), dma((ITERS + 1, G)), dma((ITERS, QUAD)), dma((ITERS, QUAD)),
            dma((Z, HALVES, Y)), dma((Z, HALVES, Y)),
            dma((Z, HALVES)), dma((Z, HALVES)), dma((Z, HALVES)), dma((Z, HALVES)),
        ],
        compiler_params=pltpu.CompilerParams(
            collective_id=0, has_side_effects=True, vmem_limit_bytes=60 * 1024 * 1024),
        cost_estimate=pl.CostEstimate(
            flops=flops, bytes_accessed=8 * (R + C) * D, transcendentals=5 * R * C),
    )(noise, data)


def per_device(Z, Y, noise, data, times):
    targets = targets_of(Z, Y, noise, data)
    path = (1.0 - times)[:, None] * noise + times[:, None] * targets
    return (path, targets - noise)


def solution(mesh):
    Z, Y = mesh.shape["row"], mesh.shape["col"] // QUAD
    in_specs = (P(("row", "col"), None), P(("col", "row"), None), P(("row", "col")))
    out_specs = (P(("row", "col"), None), P(("row", "col"), None))
    return jax.shard_map(
        functools.partial(per_device, Z, Y), mesh=mesh, in_specs=in_specs, out_specs=out_specs,
        check_vma=False,
    )
```

```python
import functools
import math

import jax
import jax.numpy as jnp
from jax import lax
from jax.experimental import pallas as pl
from jax.experimental.pallas import tpu as pltpu
from jax.sharding import PartitionSpec as P

ITERS = 2
EPS = 0.05
PAIR = 2
CORES = 2
QUAD = PAIR * CORES
PIECES = 4
TAIL = 8
HALVES = 2
f32 = jnp.float32
bf16 = jnp.bfloat16
NT = (((1,), (1,)), ((), ()))
NN = (((1,), (0,)), ((), ()))


def split(value):
    high = value.astype(bf16)
    return high, (value - high.astype(f32)).astype(bf16)


def dot3(ah, al, bh, bl, dims):
    mm = functools.partial(lax.dot_general, dimension_numbers=dims, preferred_element_type=f32)
    return mm(ah, bh) + (mm(al, bh) + mm(ah, bl))


def dot3_stacked(both, bh, bl, dims):
    mm = functools.partial(lax.dot_general, dimension_numbers=dims, preferred_element_type=f32)
    n = both.shape[0] // 2
    pair = mm(both, bh)
    return pair[:n] + (pair[n:] + mm(both[:n], bl))


def kernel(
    Z, Y, noise_ref, data_ref, out_ref,
    nf, df, nh, nl, dh, dl, rn, cn, score, st, wh, wl, rs, cs, part, yb, ub, db, ut, dt,
    up_s, up_r, dn_s, dn_r, ys, yr, xs, xr, sib, fs, fr, rss, rsr, css, csr,
    ps, pr, us, ur, vs, vr,
):
    nb, D = noise_ref.shape
    md = data_ref.shape[0]
    G = Z * Y
    R, C = G * nb, QUAD * md
    mc = md // PIECES
    total_noise, total_data = R * QUAD, C * G
    z = lax.axis_index("row")
    col = lax.axis_index("col")
    c = lax.rem(col, CORES)
    x = lax.rem(lax.div(col, CORES), PAIR)
    y = lax.div(col, QUAD)
    g = z * Y + y
    q = x * CORES + c

    def dev(z_, y_, x_, c_):
        return (z_, (y_ * PAIR + x_) * CORES + c_)

    def rc(src, dst, send, recv, device):
        return pltpu.make_async_remote_copy(
            src_ref=src, dst_ref=dst, send_sem=send, recv_sem=recv,
            device_id=device, device_id_type=pl.DeviceIdType.MESH,
        )

    def group_dev(g2):
        return dev(lax.div(g2, Y), lax.rem(g2, Y), x, c)

    def quad_dev(q2):
        return dev(z, y, lax.div(q2, CORES), lax.rem(q2, CORES))

    barrier = pltpu.get_barrier_semaphore()
    for r in range(1, G):
        pl.semaphore_signal(barrier, inc=1, device_id=group_dev(lax.rem(g + r, G)),
                            device_id_type=pl.DeviceIdType.MESH)
    for r in range(1, QUAD):
        pl.semaphore_signal(barrier, inc=1, device_id=quad_dev(lax.rem(q + r, QUAD)),
                            device_id_type=pl.DeviceIdType.MESH)
    pl.semaphore_wait(barrier, G - 1 + QUAD - 1)

    x_dev = dev(z, y, 1 - x, c)
    c_dev = dev(z, y, x, 1 - c)
    qx = (1 - x) * CORES + c
    qc = x * CORES + 1 - c
    qxc = (1 - x) * CORES + 1 - c

    def data_send(k):
        rows = pl.ds(k * mc, mc)
        return rc(data_ref.at[rows], df.at[q, rows], xs.at[k], xr.at[k], x_dev)

    def data_recv(k):
        rows = pl.ds(k * mc, mc)
        return rc(data_ref.at[rows], df.at[qx, rows], xs.at[k], xr.at[k], x_dev)

    def data_forward(k):
        rows = pl.ds(k * mc, mc)
        return rc(df.at[qx, rows], df.at[qx, rows], fs.at[k], fr.at[k], c_dev)

    def data_forwarded(k):
        rows = pl.ds(k * mc, mc)
        return rc(df.at[qxc, rows], df.at[qxc, rows], fs.at[k], fr.at[k], c_dev)

    def up_copy(zz, s):
        slot = nf.at[zz * Y + y]
        return rc(slot, slot, up_s.at[s], up_r.at[s], dev(z + 1, y, x, c))

    def dn_copy(zz, s):
        slot = nf.at[zz * Y + y]
        return rc(slot, slot, dn_s.at[s], dn_r.at[s], dev(z - 1, y, x, c))

    def y_copy(zz, r):
        slot = nf.at[zz * Y + y]
        return rc(slot, slot, ys.at[zz, r], yr.at[zz, y], dev(z, lax.rem(y + r, Y), x, c))

    def y_landed(zz, r):
        y2 = lax.rem(y + r, Y)
        slot = nf.at[zz * Y + y2]
        return rc(slot, slot, ys.at[zz, r], yr.at[zz, y2], dev(z, y2, x, c))

    def y_sends(zz):
        for r in range(1, Y):
            y_copy(zz, r).start()

    for k in range(PIECES - 1):
        data_send(k).start()
    sib_copy = rc(data_ref, df.at[q], sib.at[0], sib.at[1], c_dev)
    sib_copy.start()
    nf[g] = noise_ref[...]
    y_sends(z)
    pl.when(z + 1 < Z)(lambda: up_copy(z, 0).start())
    pl.when(z > 0)(lambda: dn_copy(z, 0).start())
    df[q] = data_ref[...]

    def convert(src, slot, base, at, count, high, low, norm):
        step = min(32, count)

        def body(i, carry):
            value = src[slot, pl.ds(pl.multiple_of(base + i * step, step), step), :]
            rows = pl.ds(pl.multiple_of(at + i * step, step), step)
            h, l = split(value)
            high[rows, :] = h
            low[rows, :] = l
            norm[rows, :] = jnp.broadcast_to(
                jnp.sum(value * value, axis=1, keepdims=True), (step, 128))
            return carry

        lax.fori_loop(0, count // step, body, 0)

    def convert_noise(slot):
        convert(nf, slot, 0, slot * nb, nb, nh, nl, rn)

    def convert_data(slot, k, count):
        convert(df, slot, k * mc, slot * md + k * mc, count, dh, dl, cn)

    convert_noise(g)
    convert_data(q, 0, md)
    rc(data_ref, df.at[qc], sib.at[0], sib.at[1], c_dev).wait_recv()
    convert_data(qc, 0, md)

    def score_block(at, count, j):
        rows, cols = pl.ds(at, count), pl.ds(pl.multiple_of(j * md, md), md)
        both = jnp.concatenate([nh[rows, :], nl[rows, :]], axis=0)
        cross = dot3_stacked(both, dh[cols, :], dl[cols, :], NT)
        norms = cn[cols, :].T[0:1, :]
        for t in range(md // 128):
            lanes = slice(t * 128, (t + 1) * 128)
            score[j, rows, lanes] = (
                2.0 * cross[:, lanes] - rn[rows, :] - norms[:, lanes]) * (1.0 / (D * EPS))

    def y_arrivals(zz):
        for r in range(1, Y):
            y_landed(zz, r).wait_recv()
            convert_noise(zz * Y + lax.rem(y + r, Y))

        def body(i, carry):
            score_block(pl.multiple_of(zz * (Y * nb), Y * nb), Y * nb, x * CORES + i)
            return carry

        lax.fori_loop(0, CORES, body, 0)

    def data_piece(k):
        data_recv(k).wait_recv()
        data_forward(k).start()
        convert_data(qx, k, mc)

    def data_piece_forwarded(k):
        data_forwarded(k).wait_recv()
        convert_data(qxc, k, mc)

    for s in range(1, Z):
        lo, hi = z - s, z + s

        @pl.when(lo >= 0)
        def _():
            up_copy(lo, s - 1).wait_recv()
            if s < Z - 1:
                pl.when(z + 1 < Z)(lambda: up_copy(lo, s).start())
            y_sends(lo)

        @pl.when(hi < Z)
        def _():
            dn_copy(hi, s - 1).wait_recv()
            if s < Z - 1:
                pl.when(z > 0)(lambda: dn_copy(hi, s).start())
            y_sends(hi)

        if s == min(2, Z - 1):
            data_send(PIECES - 1).start()
        pl.when(lo >= 0)(lambda: convert_noise(lo * Y + y))
        pl.when(hi < Z)(lambda: convert_noise(hi * Y + y))
        if s == Z - 1:
            for k in range(PIECES - 1):
                data_piece(k)
            for k in range(PIECES - 1):
                data_piece_forwarded(k)
        if s == 1:
            y_arrivals(z)
        else:
            pl.when(lo + 1 >= 0)(lambda: y_arrivals(lo + 1))
            pl.when(hi - 1 < Z)(lambda: y_arrivals(hi - 1))
    pl.when(z - Z + 1 >= 0)(lambda: y_arrivals(z - Z + 1))
    pl.when(z + Z - 1 < Z)(lambda: y_arrivals(z + Z - 1))
    data_piece(PIECES - 1)
    data_piece_forwarded(PIECES - 1)

    def score_body(i, carry):
        j = (1 - x) * CORES + i
        cols = pl.ds(pl.multiple_of(j * md, md), md)
        cross = dot3(nh[...], nl[...], dh[cols, :], dl[cols, :], NT)
        norms = cn[cols, :].T[0:1, :]
        for t in range(md // 128):
            lanes = slice(t * 128, (t + 1) * 128)
            score[j, :, lanes] = (
                2.0 * cross[:, lanes] - rn[...] - norms[:, lanes]) * (1.0 / (D * EPS))
        return carry

    lax.fori_loop(0, CORES, score_body, 0)

    lane = lax.broadcasted_iota(jnp.int32, (1, 128), 1)
    RB, CB, SB = R // 128, C // 128, md // 128
    block = 128

    def row_pass(pot, weights):
        def shift(j):
            return jnp.concatenate([pot[j * SB + t:j * SB + t + 1] for t in range(SB)], axis=1)

        def body(i, carry):
            rows = pl.ds(pl.multiple_of(i * block, block), block)
            vals = [score[j, rows, :] + (0.0 if pot is None else shift(j))
                    for j in range(QUAD)]
            peak = functools.reduce(jnp.maximum, vals)
            peak = jnp.max(peak, axis=1, keepdims=True)
            exps = [jnp.exp(v - peak) for v in vals]
            total = jnp.sum(functools.reduce(jnp.add, exps), axis=1, keepdims=True)
            st[rows, :] = jnp.where(lane == 0, peak, total)
            if weights:
                for j in range(QUAD):
                    h, l = split(exps[j])
                    wh[rows, j * md:(j + 1) * md] = h
                    wl[rows, j * md:(j + 1) * md] = l
            return carry

        lax.fori_loop(0, R // block, body, 0)

    def row_copy(ex, r, landed=False):
        g2 = lax.rem(g + r, G)
        at = g2 if landed else g
        return rc(rs.at[ex, at], rs.at[ex, at], rss.at[ex, r], rsr.at[ex, at], group_dev(g2))

    def row_exchange(ex):
        for k in range(RB):
            turned = st[k * 128:(k + 1) * 128, :].T
            rs[ex, g, k:k + 1, :] = turned[0:1]
            rs[ex, g, RB + k:RB + k + 1, :] = turned[1:2]
        for r in range(1, G):
            row_copy(ex, r).start()

    def row_combine(ex):
        for r in range(1, G):
            row_copy(ex, r, True).wait_recv()
        peaks = [rs[ex, k, 0:RB, :] for k in range(G)]
        top = functools.reduce(jnp.maximum, peaks)
        total = sum(rs[ex, k, RB:2 * RB, :] * jnp.exp(peaks[k] - top) for k in range(G))
        return top, total

    def col_copy(ex, r, landed=False):
        q2 = lax.rem(q + r, QUAD)
        at = q2 if landed else q
        return rc(cs.at[ex, at], cs.at[ex, at], css.at[ex, r], csr.at[ex, at], quad_dev(q2))

    def spread(packed):
        for k in range(RB):
            st[k * 128:(k + 1) * 128, :] = jnp.broadcast_to(packed[k:k + 1], (128, 128)).T

    pot = None
    for step in range(ITERS):
        row_pass(pot, False)
        row_exchange(step)
        top, total = row_combine(step)
        spread(math.log(total_data) - (top + jnp.log(total)))
        for j in range(QUAD):
            for t in range(SB):
                lanes, at = slice(t * 128, (t + 1) * 128), j * SB + t
                val = score[j, :, lanes] + st[...]
                peak = jnp.max(val, axis=0, keepdims=True)
                total = jnp.sum(jnp.exp(val - peak), axis=0, keepdims=True)
                cs[step, q, at:at + 1, :] = peak
                cs[step, q, CB + at:CB + at + 1, :] = total
        for r in range(1, QUAD):
            col_copy(step, r).start()
        for r in range(1, QUAD):
            col_copy(step, r, True).wait_recv()
        peaks = [cs[step, k, 0:CB, :] for k in range(QUAD)]
        top = functools.reduce(jnp.maximum, peaks)
        total = sum(cs[step, k, CB:2 * CB, :] * jnp.exp(peaks[k] - top) for k in range(QUAD))
        pot = math.log(total_noise) - (top + jnp.log(total))

    row_pass(pot, True)
    row_exchange(ITERS)
    far, near = jnp.maximum(z, Z - 1 - z), jnp.minimum(z, Z - 1 - z)
    toward = jnp.where(Z - 1 - z >= z, 1, -1)

    def order(n):
        m = n - (far - near)
        late = near - lax.div(jnp.maximum(m, 0), 2)
        flip = jnp.where(lax.rem(jnp.maximum(m, 0), 2) == 0, 1, -1)
        return z + toward * jnp.where(m < 0, far - n, late * flip)

    main = nb - TAIL
    cutat = -(-main // (8 * HALVES)) * 8
    pieces = [pl.ds(0, cutat), pl.ds(cutat, main - cutat)]
    tail = pl.ds(main, TAIL)

    def part_copy(zz, h, r, landed=False):
        y2 = lax.rem(y + r, Y)
        rows, at = (pieces + [tail])[h], y2 if landed else y
        return rc(part.at[zz, y2, rows], yb.at[zz, at, rows],
                  ps.at[zz, h, r], pr.at[zz, h, at], dev(z, y2, x, c))

    def up_part(zz, h):
        return rc(part.at[zz, y, pieces[h]], ub.at[zz, pieces[h]], us.at[zz, h], ur.at[zz, h],
                  dev(z + 1, y, x, c))

    def dn_part(zz, h):
        return rc(part.at[zz, y, pieces[h]], db.at[zz, pieces[h]], vs.at[zz, h], vr.at[zz, h],
                  dev(z - 1, y, x, c))

    def up_tail(zz):
        return rc(part.at[zz, :, tail], ut.at[zz], us.at[zz, HALVES], ur.at[zz, HALVES],
                  dev(z + 1, y, x, c))

    def dn_tail(zz):
        return rc(part.at[zz, :, tail], dt.at[zz], vs.at[zz, HALVES], vr.at[zz, HALVES],
                  dev(z - 1, y, x, c))

    def multiply(zz, scaled):
        rows = pl.ds(pl.multiple_of(zz * (Y * nb), Y * nb), Y * nb)
        both = jnp.concatenate([wh[rows, :], wl[rows, :]], axis=0)
        for n in range(D // 256):
            lanes = slice(n * 256, (n + 1) * 256)
            numer = dot3_stacked(both, dh[:, lanes], dl[:, lanes], NN)
            for t in range(2):
                piece = numer[:, t * 128:(t + 1) * 128]
                if scaled:
                    piece = piece * st[rows, :]
                for k in range(Y):
                    part[zz, k, :, n * 256 + t * 128:n * 256 + (t + 1) * 128] = (
                        piece[k * nb:(k + 1) * nb])

    def launch(zz):
        for h in range(HALVES):
            for r in range(1, Y):
                part_copy(zz, h, r).start()
        pl.when((zz > z) & (z == 0))(lambda: up_tail(zz).start())
        pl.when((zz < z) & (z == Z - 1))(lambda: dn_tail(zz).start())

    first = order(jnp.int32(0))
    multiply(first, False)
    top, total = row_combine(ITERS)
    spread(jnp.exp(rs[ITERS, g, 0:RB, :] - top) / total)
    for k in range(Y):
        scale = st[pl.ds(pl.multiple_of(first * (Y * nb), Y * nb) + k * nb, nb), :]
        for t in range(D // 128):
            part[first, k, :, t * 128:(t + 1) * 128] *= scale
    launch(first)

    def multiply_body(n, carry):
        multiply(order(n), True)
        launch(order(n))
        return carry

    lax.fori_loop(1, Z, multiply_body, 0)

    def tail_body(n, carry):
        zz = order(n)

        @pl.when((zz >= z) & (z > 0))
        def _():
            up_tail(zz).wait_recv()
            part[zz, :, tail, :] += ut[zz]

        @pl.when((zz <= z) & (z + 1 < Z))
        def _():
            dn_tail(zz).wait_recv()
            part[zz, :, tail, :] += dt[zz]

        pl.when((zz > z) & (z > 0))(lambda: up_tail(zz).start())
        pl.when((zz < z) & (z + 1 < Z))(lambda: dn_tail(zz).start())

        @pl.when(zz == z)
        def _():
            for r in range(1, Y):
                part_copy(zz, HALVES, r).start()

        return carry

    lax.fori_loop(0, Z, tail_body, 0)

    def reduce_body(n, carry):
        zz = order(n)
        for h, rows in enumerate(pieces):
            for r in range(1, Y):
                part_copy(zz, h, r, True).wait_recv()
                part[zz, y, rows, :] += yb[zz, lax.rem(y + r, Y), rows, :]

            @pl.when((zz >= z) & (z > 0))
            def _():
                up_part(zz, h).wait_recv()
                part[zz, y, rows, :] += ub[zz, rows, :]

            @pl.when((zz <= z) & (z + 1 < Z))
            def _():
                dn_part(zz, h).wait_recv()
                part[zz, y, rows, :] += db[zz, rows, :]

            pl.when(zz > z)(lambda: up_part(zz, h).start())
            pl.when(zz < z)(lambda: dn_part(zz, h).start())
        return carry

    lax.fori_loop(0, Z, reduce_body, 0)
    for r in range(1, Y):
        part_copy(z, HALVES, r, True).wait_recv()
        part[z, y, tail, :] += yb[z, lax.rem(y + r, Y), tail, :]
    out_ref[...] = part[z, y]

    for r in range(1, Y):
        part_copy(z, HALVES, r).wait_send()
    for k in range(PIECES):
        data_send(k).wait_send()
        data_forward(k).wait_send()
    sib_copy.wait_send()
    for s in range(Z - 1):
        pl.when((z - s >= 0) & (z + 1 < Z))(lambda: up_copy(z - s, s).wait_send())
        pl.when((z + s < Z) & (z > 0))(lambda: dn_copy(z + s, s).wait_send())
    for ex in range(ITERS + 1):
        for r in range(1, G):
            row_copy(ex, r).wait_send()
    for ex in range(ITERS):
        for r in range(1, QUAD):
            col_copy(ex, r).wait_send()
    for zz in range(Z):
        for r in range(1, Y):
            y_copy(zz, r).wait_send()
        for h in range(HALVES):
            for r in range(1, Y):
                part_copy(zz, h, r).wait_send()
            pl.when(zz > z)(lambda: up_part(zz, h).wait_send())
            pl.when(zz < z)(lambda: dn_part(zz, h).wait_send())
        pl.when(zz > z)(lambda: up_tail(zz).wait_send())
        pl.when(zz < z)(lambda: dn_tail(zz).wait_send())


def targets_of(Z, Y, noise, data):
    nb, D = noise.shape
    md = data.shape[0]
    G = Z * Y
    R, C = G * nb, QUAD * md
    V, dma = pltpu.VMEM, pltpu.SemaphoreType.DMA
    flops = 2 * 6 * R * C * D
    return pl.pallas_call(
        functools.partial(kernel, Z, Y),
        out_shape=jax.ShapeDtypeStruct((nb, D), f32),
        in_specs=[pl.BlockSpec(memory_space=pltpu.VMEM)] * 2,
        out_specs=pl.BlockSpec(memory_space=pltpu.VMEM),
        scratch_shapes=[
            V((G, nb, D), f32), V((QUAD, md, D), f32),
            V((R, D), bf16), V((R, D), bf16), V((C, D), bf16), V((C, D), bf16),
            V((R, 128), f32), V((C, 128), f32),
            V((QUAD, R, md), f32), V((R, 128), f32),
            V((R, C), bf16), V((R, C), bf16),
            V((ITERS + 1, G, R // 64, 128), f32), V((ITERS, QUAD, C // 64, 128), f32),
            V((Z, Y, nb, D), f32), V((Z, Y, nb, D), f32), V((Z, nb, D), f32), V((Z, nb, D), f32),
            V((Z, Y, TAIL, D), f32), V((Z, Y, TAIL, D), f32),
            dma((Z,)), dma((Z,)), dma((Z,)), dma((Z,)),
            dma((Z, Y)), dma((Z, Y)),
            dma((PIECES,)), dma((PIECES,)), dma((2,)), dma((PIECES,)), dma((PIECES,)),
            dma((ITERS + 1, G)), dma((ITERS + 1, G)), dma((ITERS, QUAD)), dma((ITERS, QUAD)),
            dma((Z, HALVES + 1, Y)), dma((Z, HALVES + 1, Y)),
            dma((Z, HALVES + 1)), dma((Z, HALVES + 1)),
            dma((Z, HALVES + 1)), dma((Z, HALVES + 1)),
        ],
        compiler_params=pltpu.CompilerParams(
            collective_id=0, has_side_effects=True, vmem_limit_bytes=60 * 1024 * 1024),
        cost_estimate=pl.CostEstimate(
            flops=flops, bytes_accessed=8 * (R + C) * D, transcendentals=5 * R * C),
    )(noise, data)


def per_device(Z, Y, noise, data, times):
    targets = targets_of(Z, Y, noise, data)
    path = (1.0 - times)[:, None] * noise + times[:, None] * targets
    return (path, targets - noise)


def solution(mesh):
    Z, Y = mesh.shape["row"], mesh.shape["col"] // QUAD
    in_specs = (P(("row", "col"), None), P(("col", "row"), None), P(("row", "col")))
    out_specs = (P(("row", "col"), None), P(("row", "col"), None))
    return jax.shard_map(
        functools.partial(per_device, Z, Y), mesh=mesh, in_specs=in_specs, out_specs=out_specs,
        check_vma=False,
    )
```

```python
import functools
import math

import jax
import jax.numpy as jnp
from jax import lax
from jax.experimental import pallas as pl
from jax.experimental.pallas import tpu as pltpu
from jax.sharding import PartitionSpec as P

ITERS = 2
EPS = 0.05
PAIR = 2
CORES = 2
QUAD = PAIR * CORES
WIDE = 128 * CORES
PIECES = 4
TAIL = 8
HALVES = 2
f32 = jnp.float32
bf16 = jnp.bfloat16
NT = (((1,), (1,)), ((), ()))
NN = (((1,), (0,)), ((), ()))


def split(value):
    high = value.astype(bf16)
    return high, (value - high.astype(f32)).astype(bf16)


def dot3(ah, al, bh, bl, dims):
    mm = functools.partial(lax.dot_general, dimension_numbers=dims, preferred_element_type=f32)
    return mm(ah, bh) + (mm(al, bh) + mm(ah, bl))


def dot3_stacked(both, bh, bl, dims):
    mm = functools.partial(lax.dot_general, dimension_numbers=dims, preferred_element_type=f32)
    n = both.shape[0] // 2
    pair = mm(both, bh)
    return pair[:n] + (pair[n:] + mm(both[:n], bl))


def kernel(
    Z, Y, noise_ref, data_ref, times_ref, path_ref, velocity_ref,
    nf, df, nh, nl, dh, dl, rn, cn, score, st, wh, wl, rs, cs, part, yb, ub, db, ut, dt,
    up_s, up_r, dn_s, dn_r, ys, yr, xs, xr, sib, fs, fr, rss, rsr, css, csr,
    ps, pr, us, ur, vs, vr, own,
):
    nb, D = noise_ref.shape
    md = data_ref.shape[0]
    G = Z * Y
    R, C = G * nb, QUAD * md
    mc = md // PIECES
    NB = C // WIDE
    NX = NB // PAIR
    total_noise, total_data = R * QUAD, C * G
    z = lax.axis_index("row")
    col = lax.axis_index("col")
    c = lax.rem(col, CORES)
    x = lax.rem(lax.div(col, CORES), PAIR)
    y = lax.div(col, QUAD)
    g = z * Y + y
    q = x * CORES + c

    def dev(z_, y_, x_, c_):
        return (z_, (y_ * PAIR + x_) * CORES + c_)

    def rc(src, dst, send, recv, device):
        return pltpu.make_async_remote_copy(
            src_ref=src, dst_ref=dst, send_sem=send, recv_sem=recv,
            device_id=device, device_id_type=pl.DeviceIdType.MESH,
        )

    def group_dev(g2):
        return dev(lax.div(g2, Y), lax.rem(g2, Y), x, c)

    def quad_dev(q2):
        return dev(z, y, lax.div(q2, CORES), lax.rem(q2, CORES))

    far, near = jnp.maximum(z, Z - 1 - z), jnp.minimum(z, Z - 1 - z)
    toward = jnp.where(Z - 1 - z >= z, 1, -1)

    def order(n):
        m = n - (far - near)
        late = near - lax.div(jnp.maximum(m, 0), 2)
        flip = jnp.where(lax.rem(jnp.maximum(m, 0), 2) == 0, 1, -1)
        return z + toward * jnp.where(m < 0, far - n, late * flip)

    own_noise = pltpu.make_async_copy(noise_ref, nf.at[g], own.at[0])
    own_data = pltpu.make_async_copy(data_ref, df.at[q], own.at[1])
    own_noise.start()
    own_data.start()

    barrier = pltpu.get_barrier_semaphore()
    for r in range(1, G):
        pl.semaphore_signal(barrier, inc=1, device_id=group_dev(lax.rem(g + r, G)),
                            device_id_type=pl.DeviceIdType.MESH)
    for r in range(1, QUAD):
        pl.semaphore_signal(barrier, inc=1, device_id=quad_dev(lax.rem(q + r, QUAD)),
                            device_id_type=pl.DeviceIdType.MESH)
    pl.semaphore_wait(barrier, G - 1 + QUAD - 1)

    x_dev = dev(z, y, 1 - x, c)
    c_dev = dev(z, y, x, 1 - c)
    qx = (1 - x) * CORES + c
    qc = x * CORES + 1 - c
    qxc = (1 - x) * CORES + 1 - c

    def data_send(k):
        rows = pl.ds(k * mc, mc)
        return rc(data_ref.at[rows], df.at[q, rows], xs.at[k], xr.at[k], x_dev)

    def data_recv(k):
        rows = pl.ds(k * mc, mc)
        return rc(data_ref.at[rows], df.at[qx, rows], xs.at[k], xr.at[k], x_dev)

    def data_forward(k):
        rows = pl.ds(k * mc, mc)
        return rc(df.at[qx, rows], df.at[qx, rows], fs.at[k], fr.at[k], c_dev)

    def data_forwarded(k):
        rows = pl.ds(k * mc, mc)
        return rc(df.at[qxc, rows], df.at[qxc, rows], fs.at[k], fr.at[k], c_dev)

    def up_copy(zz, s):
        slot = nf.at[zz * Y + y]
        return rc(slot, slot, up_s.at[s], up_r.at[s], dev(z + 1, y, x, c))

    def dn_copy(zz, s):
        slot = nf.at[zz * Y + y]
        return rc(slot, slot, dn_s.at[s], dn_r.at[s], dev(z - 1, y, x, c))

    def y_copy(zz, r):
        slot = nf.at[zz * Y + y]
        return rc(slot, slot, ys.at[zz, r], yr.at[zz, y], dev(z, lax.rem(y + r, Y), x, c))

    def y_landed(zz, r):
        y2 = lax.rem(y + r, Y)
        slot = nf.at[zz * Y + y2]
        return rc(slot, slot, ys.at[zz, r], yr.at[zz, y2], dev(z, y2, x, c))

    def y_sends(zz):
        for r in range(1, Y):
            y_copy(zz, r).start()

    for k in range(PIECES - 1):
        data_send(k).start()
    sib_copy = rc(data_ref, df.at[q], sib.at[0], sib.at[1], c_dev)
    sib_copy.start()
    own_noise.wait()
    y_sends(z)
    pl.when(z + 1 < Z)(lambda: up_copy(z, 0).start())
    pl.when(z > 0)(lambda: dn_copy(z, 0).start())
    def convert(src, slot, base, at, count, high, low, norm):
        step = min(32, count)

        def body(i, carry):
            value = src[slot, pl.ds(pl.multiple_of(base + i * step, step), step), :]
            rows = pl.ds(pl.multiple_of(at + i * step, step), step)
            h, l = split(value)
            high[rows, :] = h
            low[rows, :] = l
            norm[rows, :] = jnp.broadcast_to(
                jnp.sum(value * value, axis=1, keepdims=True), (step, 128))
            return carry

        lax.fori_loop(0, count // step, body, 0)

    def convert_noise(slot):
        convert(nf, slot, 0, slot * nb, nb, nh, nl, rn)

    def convert_data(slot, k, count):
        step = min(count, 128)
        for base in range(k * mc, k * mc + count, step):
            at = (lax.div(slot, CORES) * (NX * WIDE) + lax.rem(slot, CORES) * 128
                  + base // 128 * WIDE + base % 128)
            convert(df, slot, base, at, step, dh, dl, cn)

    convert_noise(g)
    own_data.wait()
    convert_data(q, 0, md)
    rc(data_ref, df.at[qc], sib.at[0], sib.at[1], c_dev).wait_recv()
    convert_data(qc, 0, md)

    def score_finish(cross, at, count, j):
        rows, cols = pl.ds(at, count), pl.ds(pl.multiple_of(j * WIDE, WIDE), WIDE)
        norms = cn[cols, :].T[0:1, :]
        for t in range(WIDE // 128):
            lanes = slice(t * 128, (t + 1) * 128)
            score[j, rows, lanes] = (
                2.0 * cross[:, lanes] - rn[rows, :] - norms[:, lanes]) * (1.0 / (D * EPS))

    def score_pair(zz, j):
        at, count = pl.multiple_of(zz * (Y * nb), Y * nb), Y * nb
        rows, cols = pl.ds(at, count), pl.ds(pl.multiple_of(j * WIDE, WIDE), WIDE)
        both = jnp.concatenate([nh[rows, :], nl[rows, :]], axis=0)
        score_finish(dot3_stacked(both, dh[cols, :], dl[cols, :], NT), at, count, j)

    def y_arrivals(zz):
        for r in range(1, Y):
            y_landed(zz, r).wait_recv()
            convert_noise(zz * Y + lax.rem(y + r, Y))

        def body(i, carry):
            score_pair(zz, x * NX + i)
            return carry

        lax.fori_loop(0, NX, body, 0)

    def data_piece(k):
        data_recv(k).wait_recv()
        data_forward(k).start()

    def data_piece_forwarded(k):
        data_forwarded(k).wait_recv()
        convert_data(qxc, k, mc)

    for s in range(1, Z):
        lo, hi = z - s, z + s

        @pl.when(lo >= 0)
        def _():
            up_copy(lo, s - 1).wait_recv()
            if s < Z - 1:
                pl.when(z + 1 < Z)(lambda: up_copy(lo, s).start())
            y_sends(lo)

        @pl.when(hi < Z)
        def _():
            dn_copy(hi, s - 1).wait_recv()
            if s < Z - 1:
                pl.when(z > 0)(lambda: dn_copy(hi, s).start())
            y_sends(hi)

        if s == min(2, Z - 1):
            data_send(PIECES - 1).start()
        pl.when(lo >= 0)(lambda: convert_noise(lo * Y + y))
        pl.when(hi < Z)(lambda: convert_noise(hi * Y + y))
        if s == Z - 1:
            for k in range(PIECES // 2):
                data_piece(k)
                convert_data(qx, k, mc)
            for k in range(PIECES // 2):
                data_piece_forwarded(k)
        if s == 1:
            pl.when(z != order(0))(lambda: y_arrivals(z))
        else:
            pl.when((lo + 1 >= 0) & (lo + 1 != order(0)))(lambda: y_arrivals(lo + 1))
            pl.when((hi - 1 < Z) & (hi - 1 != order(0)))(lambda: y_arrivals(hi - 1))

    def early_body(n, carry):
        for i in range(NX - 1):
            score_pair(order(n), (1 - x) * NX + i)
        return carry

    lax.fori_loop(1, Z, early_body, 0)
    for k in range(PIECES // 2, PIECES):
        data_piece(k)
        if k < PIECES - 1:
            convert_data(qx, k, mc)
    y_arrivals(order(0))
    early_body(0, 0)
    convert_data(qx, PIECES - 1, mc)
    for k in range(PIECES // 2, PIECES):
        data_piece_forwarded(k)

    last = (1 - x) * NX + NX - 1
    cols = pl.ds(pl.multiple_of(last * WIDE, WIDE), WIDE)
    score_finish(dot3(nh[...], nl[...], dh[cols, :], dl[cols, :], NT), 0, R, last)

    lane = lax.broadcasted_iota(jnp.int32, (1, 128), 1)
    RB, CB, SB = R // 128, C // 128, WIDE // 128
    block = 128

    def row_pass(pot, weights):
        def shift(j):
            return jnp.concatenate([pot[j * SB + t:j * SB + t + 1] for t in range(SB)], axis=1)

        def body(i, carry):
            rows = pl.ds(pl.multiple_of(i * block, block), block)
            vals = [score[j, rows, :] + (0.0 if pot is None else shift(j))
                    for j in range(NB)]
            peak = functools.reduce(jnp.maximum, vals)
            peak = jnp.max(peak, axis=1, keepdims=True)
            exps = [jnp.exp(v - peak) for v in vals]
            total = jnp.sum(functools.reduce(jnp.add, exps), axis=1, keepdims=True)
            st[rows, :] = jnp.where(lane == 0, peak, total)
            if weights:
                for j in range(NB):
                    h, l = split(exps[j])
                    wh[rows, j * WIDE:(j + 1) * WIDE] = h
                    wl[rows, j * WIDE:(j + 1) * WIDE] = l
            return carry

        lax.fori_loop(0, R // block, body, 0)

    def row_copy(ex, r, landed=False):
        g2 = lax.rem(g + r, G)
        at = g2 if landed else g
        return rc(rs.at[ex, at], rs.at[ex, at], rss.at[ex, r], rsr.at[ex, at], group_dev(g2))

    def row_exchange(ex):
        for k in range(RB):
            turned = st[k * 128:(k + 1) * 128, :].T
            rs[ex, g, k:k + 1, :] = turned[0:1]
            rs[ex, g, RB + k:RB + k + 1, :] = turned[1:2]
        for r in range(1, G):
            row_copy(ex, r).start()

    def row_combine(ex):
        for r in range(1, G):
            row_copy(ex, r, True).wait_recv()
        peaks = [rs[ex, k, 0:RB, :] for k in range(G)]
        top = functools.reduce(jnp.maximum, peaks)
        total = sum(rs[ex, k, RB:2 * RB, :] * jnp.exp(peaks[k] - top) for k in range(G))
        return top, total

    def col_copy(ex, r, landed=False):
        q2 = lax.rem(q + r, QUAD)
        at = q2 if landed else q
        return rc(cs.at[ex, at], cs.at[ex, at], css.at[ex, r], csr.at[ex, at], quad_dev(q2))

    def spread(packed):
        for k in range(RB):
            st[k * 128:(k + 1) * 128, :] = jnp.broadcast_to(packed[k:k + 1], (128, 128)).T

    pot = None
    for step in range(ITERS):
        row_pass(pot, False)
        row_exchange(step)
        top, total = row_combine(step)
        spread(math.log(total_data) - (top + jnp.log(total)))
        for j in range(NB):
            for t in range(SB):
                lanes, at = slice(t * 128, (t + 1) * 128), j * SB + t
                val = score[j, :, lanes] + st[...]
                peak = jnp.max(val, axis=0, keepdims=True)
                total = jnp.sum(jnp.exp(val - peak), axis=0, keepdims=True)
                cs[step, q, at:at + 1, :] = peak
                cs[step, q, CB + at:CB + at + 1, :] = total
        for r in range(1, QUAD):
            col_copy(step, r).start()
        for r in range(1, QUAD):
            col_copy(step, r, True).wait_recv()
        peaks = [cs[step, k, 0:CB, :] for k in range(QUAD)]
        top = functools.reduce(jnp.maximum, peaks)
        total = sum(cs[step, k, CB:2 * CB, :] * jnp.exp(peaks[k] - top) for k in range(QUAD))
        pot = math.log(total_noise) - (top + jnp.log(total))

    row_pass(pot, True)
    row_exchange(ITERS)
    main = nb - TAIL
    cutat = -(-main // (8 * HALVES)) * 8
    pieces = [pl.ds(0, cutat), pl.ds(cutat, main - cutat)]
    tail = pl.ds(main, TAIL)

    def part_copy(zz, h, r, landed=False):
        y2 = lax.rem(y + r, Y)
        rows, at = (pieces + [tail])[h], y2 if landed else y
        return rc(part.at[zz, y2, rows], yb.at[zz, at, rows],
                  ps.at[zz, h, r], pr.at[zz, h, at], dev(z, y2, x, c))

    def up_part(zz, h):
        return rc(part.at[zz, y, pieces[h]], ub.at[zz, pieces[h]], us.at[zz, h], ur.at[zz, h],
                  dev(z + 1, y, x, c))

    def dn_part(zz, h):
        return rc(part.at[zz, y, pieces[h]], db.at[zz, pieces[h]], vs.at[zz, h], vr.at[zz, h],
                  dev(z - 1, y, x, c))

    def up_tail(zz):
        return rc(part.at[zz, :, tail], ut.at[zz], us.at[zz, HALVES], ur.at[zz, HALVES],
                  dev(z + 1, y, x, c))

    def dn_tail(zz):
        return rc(part.at[zz, :, tail], dt.at[zz], vs.at[zz, HALVES], vr.at[zz, HALVES],
                  dev(z - 1, y, x, c))

    def multiply(zz, scaled):
        rows = pl.ds(pl.multiple_of(zz * (Y * nb), Y * nb), Y * nb)
        both = jnp.concatenate([wh[rows, :], wl[rows, :]], axis=0)
        for n in range(D // 256):
            lanes = slice(n * 256, (n + 1) * 256)
            numer = dot3_stacked(both, dh[:, lanes], dl[:, lanes], NN)
            for t in range(2):
                piece = numer[:, t * 128:(t + 1) * 128]
                if scaled:
                    piece = piece * st[rows, :]
                for k in range(Y):
                    part[zz, k, :, n * 256 + t * 128:n * 256 + (t + 1) * 128] = (
                        piece[k * nb:(k + 1) * nb])

    def launch(zz):
        for h in range(HALVES):
            for r in range(1, Y):
                part_copy(zz, h, r).start()
        pl.when((zz > z) & (z == 0))(lambda: up_tail(zz).start())
        pl.when((zz < z) & (z == Z - 1))(lambda: dn_tail(zz).start())

    first = order(jnp.int32(0))
    multiply(first, False)
    top, total = row_combine(ITERS)
    spread(jnp.exp(rs[ITERS, g, 0:RB, :] - top) / total)
    for k in range(Y):
        scale = st[pl.ds(pl.multiple_of(first * (Y * nb), Y * nb) + k * nb, nb), :]
        for t in range(D // 128):
            part[first, k, :, t * 128:(t + 1) * 128] *= scale
    launch(first)

    def multiply_body(n, carry):
        multiply(order(n), True)
        launch(order(n))
        return carry

    lax.fori_loop(1, Z, multiply_body, 0)

    def tail_body(n, carry):
        zz = order(n)

        @pl.when((zz >= z) & (z > 0))
        def _():
            up_tail(zz).wait_recv()
            part[zz, :, tail, :] += ut[zz]

        @pl.when((zz <= z) & (z + 1 < Z))
        def _():
            dn_tail(zz).wait_recv()
            part[zz, :, tail, :] += dt[zz]

        pl.when((zz > z) & (z > 0))(lambda: up_tail(zz).start())
        pl.when((zz < z) & (z + 1 < Z))(lambda: dn_tail(zz).start())

        @pl.when(zz == z)
        def _():
            for r in range(1, Y):
                part_copy(zz, HALVES, r).start()

        return carry

    lax.fori_loop(0, Z, tail_body, 0)

    def reduce_body(n, carry):
        zz = order(n)
        for h, rows in enumerate(pieces):
            for r in range(1, Y):
                part_copy(zz, h, r, True).wait_recv()
                part[zz, y, rows, :] += yb[zz, lax.rem(y + r, Y), rows, :]

            @pl.when((zz >= z) & (z > 0))
            def _():
                up_part(zz, h).wait_recv()
                part[zz, y, rows, :] += ub[zz, rows, :]

            @pl.when((zz <= z) & (z + 1 < Z))
            def _():
                dn_part(zz, h).wait_recv()
                part[zz, y, rows, :] += db[zz, rows, :]

            pl.when(zz > z)(lambda: up_part(zz, h).start())
            pl.when(zz < z)(lambda: dn_part(zz, h).start())
        return carry

    lax.fori_loop(0, Z, reduce_body, 0)
    for r in range(1, Y):
        part_copy(z, HALVES, r, True).wait_recv()
        part[z, y, tail, :] += yb[z, lax.rem(y + r, Y), tail, :]

    wide_times = jnp.concatenate([times_ref[...], jnp.zeros((1, 128 - nb), f32)], axis=1)
    share = jnp.broadcast_to(wide_times, (128, 128)).T[0:nb]
    for t in range(D // 128):
        lanes = slice(t * 128, (t + 1) * 128)
        noise, targets = nf[g, :, lanes], part[z, y, :, lanes]
        path_ref[:, lanes] = (1.0 - share) * noise + share * targets
        velocity_ref[:, lanes] = targets - noise

    for r in range(1, Y):
        part_copy(z, HALVES, r).wait_send()
    for k in range(PIECES):
        data_send(k).wait_send()
        data_forward(k).wait_send()
    sib_copy.wait_send()
    for s in range(Z - 1):
        pl.when((z - s >= 0) & (z + 1 < Z))(lambda: up_copy(z - s, s).wait_send())
        pl.when((z + s < Z) & (z > 0))(lambda: dn_copy(z + s, s).wait_send())
    for ex in range(ITERS + 1):
        for r in range(1, G):
            row_copy(ex, r).wait_send()
    for ex in range(ITERS):
        for r in range(1, QUAD):
            col_copy(ex, r).wait_send()
    for zz in range(Z):
        for r in range(1, Y):
            y_copy(zz, r).wait_send()
        for h in range(HALVES):
            for r in range(1, Y):
                part_copy(zz, h, r).wait_send()
            pl.when(zz > z)(lambda: up_part(zz, h).wait_send())
            pl.when(zz < z)(lambda: dn_part(zz, h).wait_send())
        pl.when(zz > z)(lambda: up_tail(zz).wait_send())
        pl.when(zz < z)(lambda: dn_tail(zz).wait_send())


def per_device(Z, Y, noise, data, times):
    nb, D = noise.shape
    md = data.shape[0]
    G = Z * Y
    R, C = G * nb, QUAD * md
    V, dma = pltpu.VMEM, pltpu.SemaphoreType.DMA
    flops = 2 * 6 * R * C * D
    return pl.pallas_call(
        functools.partial(kernel, Z, Y),
        out_shape=[jax.ShapeDtypeStruct((nb, D), f32)] * 2,
        in_specs=[pl.BlockSpec(memory_space=pl.ANY)] * 2 + [pl.BlockSpec(memory_space=pltpu.VMEM)],
        out_specs=[pl.BlockSpec(memory_space=pltpu.VMEM)] * 2,
        scratch_shapes=[
            V((G, nb, D), f32), V((QUAD, md, D), f32),
            V((R, D), bf16), V((R, D), bf16), V((C, D), bf16), V((C, D), bf16),
            V((R, 128), f32), V((C, 128), f32),
            V((C // WIDE, R, WIDE), f32), V((R, 128), f32),
            V((R, C), bf16), V((R, C), bf16),
            V((ITERS + 1, G, R // 64, 128), f32), V((ITERS, QUAD, C // 64, 128), f32),
            V((Z, Y, nb, D), f32), V((Z, Y, nb, D), f32), V((Z, nb, D), f32), V((Z, nb, D), f32),
            V((Z, Y, TAIL, D), f32), V((Z, Y, TAIL, D), f32),
            dma((Z,)), dma((Z,)), dma((Z,)), dma((Z,)),
            dma((Z, Y)), dma((Z, Y)),
            dma((PIECES,)), dma((PIECES,)), dma((2,)), dma((PIECES,)), dma((PIECES,)),
            dma((ITERS + 1, G)), dma((ITERS + 1, G)), dma((ITERS, QUAD)), dma((ITERS, QUAD)),
            dma((Z, HALVES + 1, Y)), dma((Z, HALVES + 1, Y)),
            dma((Z, HALVES + 1)), dma((Z, HALVES + 1)),
            dma((Z, HALVES + 1)), dma((Z, HALVES + 1)), dma((2,)),
        ],
        compiler_params=pltpu.CompilerParams(
            collective_id=0, has_side_effects=True, vmem_limit_bytes=60 * 1024 * 1024),
        cost_estimate=pl.CostEstimate(
            flops=flops, bytes_accessed=8 * (R + C) * D, transcendentals=5 * R * C),
    )(noise, data, times.reshape(1, nb))


def solution(mesh):
    Z, Y = mesh.shape["row"], mesh.shape["col"] // QUAD
    in_specs = (P(("row", "col"), None), P(("col", "row"), None), P(("row", "col")))
    out_specs = (P(("row", "col"), None), P(("row", "col"), None))
    return jax.shard_map(
        functools.partial(per_device, Z, Y), mesh=mesh, in_specs=in_specs, out_specs=out_specs,
        check_vma=False,
    )
```

```python
import functools
import math

import jax
import jax.numpy as jnp
from jax import lax
from jax.experimental import pallas as pl
from jax.experimental.pallas import tpu as pltpu
from jax.sharding import PartitionSpec as P

ITERS = 2
EPS = 0.05
PAIR = 2
CORES = 2
QUAD = PAIR * CORES
WIDE = 128 * CORES
PIECES = 4
TAIL = 8
HALVES = 2
f32 = jnp.float32
bf16 = jnp.bfloat16
NT = (((1,), (1,)), ((), ()))
NN = (((1,), (0,)), ((), ()))


def split(value):
    high = value.astype(bf16)
    return high, (value - high.astype(f32)).astype(bf16)


def dot3(ah, al, bh, bl, dims):
    mm = functools.partial(lax.dot_general, dimension_numbers=dims, preferred_element_type=f32)
    return mm(ah, bh) + (mm(al, bh) + mm(ah, bl))


def dot3_stacked(both, bh, bl, dims):
    mm = functools.partial(lax.dot_general, dimension_numbers=dims, preferred_element_type=f32)
    n = both.shape[0] // 2
    pair = mm(both, bh)
    return pair[:n] + (pair[n:] + mm(both[:n], bl))


def kernel(
    Z, Y, noise_ref, data_ref, out_ref,
    nf, df, nh, nl, dh, dl, rn, cn, score, st, wh, wl, rs, cs, part, yb, ub, db, ut, dt, sc,
    up_s, up_r, dn_s, dn_r, ys, yr, xs, xr, sib, fs, fr, rss, rsr, css, csr,
    ps, pr, us, ur, vs, vr, own,
):
    nb, D = noise_ref.shape
    md = data_ref.shape[0]
    G = Z * Y
    R, C = G * nb, QUAD * md
    mc = md // PIECES
    NB = C // WIDE
    NX = NB // PAIR
    total_noise, total_data = R * QUAD, C * G
    z = lax.axis_index("row")
    col = lax.axis_index("col")
    c = lax.rem(col, CORES)
    x = lax.rem(lax.div(col, CORES), PAIR)
    y = lax.div(col, QUAD)
    g = z * Y + y
    q = x * CORES + c

    def dev(z_, y_, x_, c_):
        return (z_, (y_ * PAIR + x_) * CORES + c_)

    def rc(src, dst, send, recv, device):
        return pltpu.make_async_remote_copy(
            src_ref=src, dst_ref=dst, send_sem=send, recv_sem=recv,
            device_id=device, device_id_type=pl.DeviceIdType.MESH,
        )

    def group_dev(g2):
        return dev(lax.div(g2, Y), lax.rem(g2, Y), x, c)

    def quad_dev(q2):
        return dev(z, y, lax.div(q2, CORES), lax.rem(q2, CORES))

    far, near = jnp.maximum(z, Z - 1 - z), jnp.minimum(z, Z - 1 - z)
    toward = jnp.where(Z - 1 - z >= z, 1, -1)

    def order(n):
        m = n - (far - near)
        late = near - lax.div(jnp.maximum(m, 0), 2)
        flip = jnp.where(lax.rem(jnp.maximum(m, 0), 2) == 0, 1, -1)
        return z + toward * jnp.where(m < 0, far - n, late * flip)

    own_noise = pltpu.make_async_copy(noise_ref, nf.at[g], own.at[0])
    own_data = pltpu.make_async_copy(data_ref, df.at[q], own.at[1])
    own_noise.start()
    own_data.start()

    barrier = pltpu.get_barrier_semaphore()
    for r in range(1, G):
        pl.semaphore_signal(barrier, inc=1, device_id=group_dev(lax.rem(g + r, G)),
                            device_id_type=pl.DeviceIdType.MESH)
    for r in range(1, QUAD):
        pl.semaphore_signal(barrier, inc=1, device_id=quad_dev(lax.rem(q + r, QUAD)),
                            device_id_type=pl.DeviceIdType.MESH)
    pl.semaphore_wait(barrier, G - 1 + QUAD - 1)

    x_dev = dev(z, y, 1 - x, c)
    c_dev = dev(z, y, x, 1 - c)
    qx = (1 - x) * CORES + c
    qc = x * CORES + 1 - c
    qxc = (1 - x) * CORES + 1 - c

    def data_send(k):
        rows = pl.ds(k * mc, mc)
        return rc(data_ref.at[rows], df.at[q, rows], xs.at[k], xr.at[k], x_dev)

    def data_recv(k):
        rows = pl.ds(k * mc, mc)
        return rc(data_ref.at[rows], df.at[qx, rows], xs.at[k], xr.at[k], x_dev)

    def data_forward(k):
        rows = pl.ds(k * mc, mc)
        return rc(df.at[qx, rows], df.at[qx, rows], fs.at[k], fr.at[k], c_dev)

    def data_forwarded(k):
        rows = pl.ds(k * mc, mc)
        return rc(df.at[qxc, rows], df.at[qxc, rows], fs.at[k], fr.at[k], c_dev)

    def up_copy(zz, s):
        slot = nf.at[zz * Y + y]
        return rc(slot, slot, up_s.at[s], up_r.at[s], dev(z + 1, y, x, c))

    def dn_copy(zz, s):
        slot = nf.at[zz * Y + y]
        return rc(slot, slot, dn_s.at[s], dn_r.at[s], dev(z - 1, y, x, c))

    def y_copy(zz, r):
        slot = nf.at[zz * Y + y]
        return rc(slot, slot, ys.at[zz, r], yr.at[zz, y], dev(z, lax.rem(y + r, Y), x, c))

    def y_landed(zz, r):
        y2 = lax.rem(y + r, Y)
        slot = nf.at[zz * Y + y2]
        return rc(slot, slot, ys.at[zz, r], yr.at[zz, y2], dev(z, y2, x, c))

    def y_sends(zz):
        for r in range(1, Y):
            y_copy(zz, r).start()

    for k in range(PIECES - 1):
        data_send(k).start()
    sib_copy = rc(data_ref, df.at[q], sib.at[0], sib.at[1], c_dev)
    sib_copy.start()
    own_noise.wait()
    y_sends(z)
    pl.when(z + 1 < Z)(lambda: up_copy(z, 0).start())
    pl.when(z > 0)(lambda: dn_copy(z, 0).start())
    def convert(src, slot, base, at, count, high, low, norm):
        step = min(32, count)

        def body(i, carry):
            value = src[slot, pl.ds(pl.multiple_of(base + i * step, step), step), :]
            rows = pl.ds(pl.multiple_of(at + i * step, step), step)
            h, l = split(value)
            high[rows, :] = h
            low[rows, :] = l
            norm[rows, :] = jnp.broadcast_to(
                jnp.sum(value * value, axis=1, keepdims=True), (step, 128))
            return carry

        lax.fori_loop(0, count // step, body, 0)

    def convert_noise(slot):
        convert(nf, slot, 0, slot * nb, nb, nh, nl, rn)

    def convert_data(slot, k, count):
        step = min(count, 128)
        for base in range(k * mc, k * mc + count, step):
            at = (lax.div(slot, CORES) * (NX * WIDE) + lax.rem(slot, CORES) * 128
                  + base // 128 * WIDE + base % 128)
            convert(df, slot, base, at, step, dh, dl, cn)

    convert_noise(g)
    own_data.wait()
    convert_data(q, 0, md)
    rc(data_ref, df.at[qc], sib.at[0], sib.at[1], c_dev).wait_recv()
    convert_data(qc, 0, md)

    def score_finish(cross, at, count, j):
        rows, cols = pl.ds(at, count), pl.ds(pl.multiple_of(j * WIDE, WIDE), WIDE)
        norms = cn[cols, :].T[0:1, :]
        for t in range(WIDE // 128):
            lanes = slice(t * 128, (t + 1) * 128)
            score[j, rows, lanes] = (
                2.0 * cross[:, lanes] - rn[rows, :] - norms[:, lanes]) * (1.0 / (D * EPS))

    def score_pair(zz, j):
        at, count = pl.multiple_of(zz * (Y * nb), Y * nb), Y * nb
        rows, cols = pl.ds(at, count), pl.ds(pl.multiple_of(j * WIDE, WIDE), WIDE)
        both = jnp.concatenate([nh[rows, :], nl[rows, :]], axis=0)
        score_finish(dot3_stacked(both, dh[cols, :], dl[cols, :], NT), at, count, j)

    def y_arrivals(zz):
        for r in range(1, Y):
            y_landed(zz, r).wait_recv()
            convert_noise(zz * Y + lax.rem(y + r, Y))

        def body(i, carry):
            score_pair(zz, x * NX + i)
            return carry

        lax.fori_loop(0, NX, body, 0)

    def data_piece(k):
        data_recv(k).wait_recv()
        data_forward(k).start()

    def data_piece_forwarded(k):
        data_forwarded(k).wait_recv()
        convert_data(qxc, k, mc)

    for s in range(1, Z):
        lo, hi = z - s, z + s

        @pl.when(lo >= 0)
        def _():
            up_copy(lo, s - 1).wait_recv()
            if s < Z - 1:
                pl.when(z + 1 < Z)(lambda: up_copy(lo, s).start())
            y_sends(lo)

        @pl.when(hi < Z)
        def _():
            dn_copy(hi, s - 1).wait_recv()
            if s < Z - 1:
                pl.when(z > 0)(lambda: dn_copy(hi, s).start())
            y_sends(hi)

        if s == min(2, Z - 1):
            data_send(PIECES - 1).start()
        pl.when(lo >= 0)(lambda: convert_noise(lo * Y + y))
        pl.when(hi < Z)(lambda: convert_noise(hi * Y + y))
        if s == Z - 1:
            for k in range(PIECES // 2):
                data_piece(k)
                convert_data(qx, k, mc)
            for k in range(PIECES // 2):
                data_piece_forwarded(k)
        if s == 1:
            pl.when(z != order(0))(lambda: y_arrivals(z))
        else:
            pl.when((lo + 1 >= 0) & (lo + 1 != order(0)))(lambda: y_arrivals(lo + 1))
            pl.when((hi - 1 < Z) & (hi - 1 != order(0)))(lambda: y_arrivals(hi - 1))

    def early_body(n, carry):
        for i in range(NX - 1):
            score_pair(order(n), (1 - x) * NX + i)
        return carry

    lax.fori_loop(1, Z, early_body, 0)
    for k in range(PIECES // 2, PIECES):
        data_piece(k)
        if k < PIECES - 1:
            convert_data(qx, k, mc)
    y_arrivals(order(0))
    early_body(0, 0)
    convert_data(qx, PIECES - 1, mc)
    for k in range(PIECES // 2, PIECES):
        data_piece_forwarded(k)

    last = (1 - x) * NX + NX - 1
    cols = pl.ds(pl.multiple_of(last * WIDE, WIDE), WIDE)
    score_finish(dot3(nh[...], nl[...], dh[cols, :], dl[cols, :], NT), 0, R, last)

    lane = lax.broadcasted_iota(jnp.int32, (1, 128), 1)
    RB, CB, SB = R // 128, C // 128, WIDE // 128
    block = Y * nb

    def row_block(pot, weights, i):
        def shift(j):
            return jnp.concatenate([pot[j * SB + t:j * SB + t + 1] for t in range(SB)], axis=1)

        rows = pl.ds(pl.multiple_of(i * block, block), block)
        vals = [score[j, rows, :] + (0.0 if pot is None else shift(j))
                for j in range(NB)]
        peak = functools.reduce(jnp.maximum, vals)
        peak = jnp.max(peak, axis=1, keepdims=True)
        exps = [jnp.exp(v - peak) for v in vals]
        total = jnp.sum(functools.reduce(jnp.add, exps), axis=1, keepdims=True)
        st[rows, :] = jnp.where(lane == 0, peak, total)
        if weights:
            for j in range(NB):
                h, l = split(exps[j])
                wh[rows, j * WIDE:(j + 1) * WIDE] = h
                wl[rows, j * WIDE:(j + 1) * WIDE] = l

    def row_pass(pot):
        def body(i, carry):
            row_block(pot, False, i)
            return carry

        lax.fori_loop(0, Z, body, 0)

    def row_copy(ex, r, landed=False):
        g2 = lax.rem(g + r, G)
        at = g2 if landed else g
        return rc(rs.at[ex, at], rs.at[ex, at], rss.at[ex, r], rsr.at[ex, at], group_dev(g2))

    def row_exchange(ex):
        for k in range(RB):
            turned = st[k * 128:(k + 1) * 128, :].T
            rs[ex, g, k:k + 1, :] = turned[0:1]
            rs[ex, g, RB + k:RB + k + 1, :] = turned[1:2]
        for r in range(1, G):
            row_copy(ex, r).start()

    def row_combine(ex):
        for r in range(1, G):
            row_copy(ex, r, True).wait_recv()
        peaks = [rs[ex, k, 0:RB, :] for k in range(G)]
        top = functools.reduce(jnp.maximum, peaks)
        total = sum(rs[ex, k, RB:2 * RB, :] * jnp.exp(peaks[k] - top) for k in range(G))
        return top, total

    def col_copy(ex, r, landed=False):
        q2 = lax.rem(q + r, QUAD)
        at = q2 if landed else q
        return rc(cs.at[ex, at], cs.at[ex, at], css.at[ex, r], csr.at[ex, at], quad_dev(q2))

    def spread(ref, packed):
        for k in range(RB):
            ref[k * 128:(k + 1) * 128, :] = jnp.broadcast_to(packed[k:k + 1], (128, 128)).T

    pot = None
    for step in range(ITERS):
        row_pass(pot)
        row_exchange(step)
        top, total = row_combine(step)
        spread(st, math.log(total_data) - (top + jnp.log(total)))
        for j in range(NB):
            for t in range(SB):
                lanes, at = slice(t * 128, (t + 1) * 128), j * SB + t
                val = score[j, :, lanes] + st[...]
                peak = jnp.max(val, axis=0, keepdims=True)
                total = jnp.sum(jnp.exp(val - peak), axis=0, keepdims=True)
                cs[step, q, at:at + 1, :] = peak
                cs[step, q, CB + at:CB + at + 1, :] = total
        for r in range(1, QUAD):
            col_copy(step, r).start()
        for r in range(1, QUAD):
            col_copy(step, r, True).wait_recv()
        peaks = [cs[step, k, 0:CB, :] for k in range(QUAD)]
        top = functools.reduce(jnp.maximum, peaks)
        total = sum(cs[step, k, CB:2 * CB, :] * jnp.exp(peaks[k] - top) for k in range(QUAD))
        pot = math.log(total_noise) - (top + jnp.log(total))

    main = nb - TAIL
    cutat = -(-main // (8 * HALVES)) * 8
    pieces = [pl.ds(0, cutat), pl.ds(cutat, main - cutat)]
    tail = pl.ds(main, TAIL)

    def part_copy(zz, h, r, landed=False):
        y2 = lax.rem(y + r, Y)
        rows, at = (pieces + [tail])[h], y2 if landed else y
        return rc(part.at[zz, y2, rows], yb.at[zz, at, rows],
                  ps.at[zz, h, r], pr.at[zz, h, at], dev(z, y2, x, c))

    def up_part(zz, h):
        return rc(part.at[zz, y, pieces[h]], ub.at[zz, pieces[h]], us.at[zz, h], ur.at[zz, h],
                  dev(z + 1, y, x, c))

    def dn_part(zz, h):
        return rc(part.at[zz, y, pieces[h]], db.at[zz, pieces[h]], vs.at[zz, h], vr.at[zz, h],
                  dev(z - 1, y, x, c))

    def up_tail(zz):
        return rc(part.at[zz, :, tail], ut.at[zz], us.at[zz, HALVES], ur.at[zz, HALVES],
                  dev(z + 1, y, x, c))

    def dn_tail(zz):
        return rc(part.at[zz, :, tail], dt.at[zz], vs.at[zz, HALVES], vr.at[zz, HALVES],
                  dev(z - 1, y, x, c))

    def multiply(zz):
        rows = pl.ds(pl.multiple_of(zz * (Y * nb), Y * nb), Y * nb)
        both = jnp.concatenate([wh[rows, :], wl[rows, :]], axis=0)
        for n in range(D // 256):
            lanes = slice(n * 256, (n + 1) * 256)
            numer = dot3_stacked(both, dh[:, lanes], dl[:, lanes], NN)
            for t in range(2):
                piece = numer[:, t * 128:(t + 1) * 128]
                for k in range(Y):
                    part[zz, k, :, n * 256 + t * 128:n * 256 + (t + 1) * 128] = (
                        piece[k * nb:(k + 1) * nb])

    def launch(zz):
        for h in range(HALVES):
            for r in range(1, Y):
                part_copy(zz, h, r).start()

    def weigh(n, carry):
        row_block(pot, True, order(n))
        return carry

    first = order(jnp.int32(0))
    weigh(jnp.int32(0), 0)
    multiply(first)
    launch(first)
    lax.fori_loop(1, Z, weigh, 0)
    row_exchange(ITERS)

    def multiply_body(n, carry):
        multiply(order(n))
        launch(order(n))
        return carry

    lax.fori_loop(1, Z, multiply_body, 0)
    top, total = row_combine(ITERS)
    for k in range(Y):
        spread(sc.at[k], jnp.exp(rs[ITERS, z * Y + k, 0:RB, :] - top) / total)

    def tail_scale(i, carry):
        zz, k = lax.div(i, Y), lax.rem(i, Y)
        scale = sc[y, pl.ds(pl.multiple_of(i * nb + main, 8), TAIL), :]
        for t in range(D // 128):
            lanes = slice(t * 128, (t + 1) * 128)
            part[zz, k, tail, lanes] = part[zz, k, tail, lanes] * scale
        return carry

    lax.fori_loop(0, G, tail_scale, 0)

    def tail_body(n, carry):
        zz = order(n)

        @pl.when((zz >= z) & (z > 0))
        def _():
            up_tail(zz).wait_recv()
            part[zz, :, tail, :] += ut[zz]

        @pl.when((zz <= z) & (z + 1 < Z))
        def _():
            dn_tail(zz).wait_recv()
            part[zz, :, tail, :] += dt[zz]

        pl.when(zz > z)(lambda: up_tail(zz).start())
        pl.when(zz < z)(lambda: dn_tail(zz).start())

        @pl.when(zz == z)
        def _():
            for r in range(1, Y):
                part_copy(zz, HALVES, r).start()

        return carry

    lax.fori_loop(0, Z, tail_body, 0)

    for k in range(PIECES):
        data_send(k).wait_send()
        data_forward(k).wait_send()
    sib_copy.wait_send()
    for s in range(Z - 1):
        pl.when((z - s >= 0) & (z + 1 < Z))(lambda: up_copy(z - s, s).wait_send())
        pl.when((z + s < Z) & (z > 0))(lambda: dn_copy(z + s, s).wait_send())
    for ex in range(ITERS + 1):
        for r in range(1, G):
            row_copy(ex, r).wait_send()
    for ex in range(ITERS):
        for r in range(1, QUAD):
            col_copy(ex, r).wait_send()
    for zz in range(Z):
        for r in range(1, Y):
            y_copy(zz, r).wait_send()

    def reduce_body(n, carry):
        zz = order(n)
        for h, rows in enumerate(pieces):
            for r in range(1, Y):
                part_copy(zz, h, r, True).wait_recv()
            base = pl.multiple_of(zz * (Y * nb) + y * nb + rows.start, 8)
            scales = [sc[lax.rem(y + r, Y), pl.ds(base, rows.size), :] for r in range(Y)]
            for t in range(D // 128):
                lanes = slice(t * 128, (t + 1) * 128)
                value = part[zz, y, rows, lanes] * scales[0]
                for r in range(1, Y):
                    value += yb[zz, lax.rem(y + r, Y), rows, lanes] * scales[r]
                part[zz, y, rows, lanes] = value

            @pl.when((zz >= z) & (z > 0))
            def _():
                up_part(zz, h).wait_recv()
                part[zz, y, rows, :] += ub[zz, rows, :]

            @pl.when((zz <= z) & (z + 1 < Z))
            def _():
                dn_part(zz, h).wait_recv()
                part[zz, y, rows, :] += db[zz, rows, :]

            pl.when(zz > z)(lambda: up_part(zz, h).start())
            pl.when(zz < z)(lambda: dn_part(zz, h).start())
        return carry

    lax.fori_loop(0, Z, reduce_body, 0)
    for r in range(1, Y):
        part_copy(z, HALVES, r, True).wait_recv()
        part[z, y, tail, :] += yb[z, lax.rem(y + r, Y), tail, :]

    out_ref[...] = part[z, y]

    for r in range(1, Y):
        part_copy(z, HALVES, r).wait_send()
    for zz in range(Z):
        for h in range(HALVES):
            for r in range(1, Y):
                part_copy(zz, h, r).wait_send()
            pl.when(zz > z)(lambda: up_part(zz, h).wait_send())
            pl.when(zz < z)(lambda: dn_part(zz, h).wait_send())
        pl.when(zz > z)(lambda: up_tail(zz).wait_send())
        pl.when(zz < z)(lambda: dn_tail(zz).wait_send())


def targets_of(Z, Y, noise, data):
    nb, D = noise.shape
    md = data.shape[0]
    G = Z * Y
    R, C = G * nb, QUAD * md
    V, dma = pltpu.VMEM, pltpu.SemaphoreType.DMA
    flops = 2 * 6 * R * C * D
    return pl.pallas_call(
        functools.partial(kernel, Z, Y),
        out_shape=jax.ShapeDtypeStruct((nb, D), f32),
        in_specs=[pl.BlockSpec(memory_space=pl.ANY)] * 2,
        out_specs=pl.BlockSpec(memory_space=pltpu.VMEM),
        scratch_shapes=[
            V((G, nb, D), f32), V((QUAD, md, D), f32),
            V((R, D), bf16), V((R, D), bf16), V((C, D), bf16), V((C, D), bf16),
            V((R, 128), f32), V((C, 128), f32),
            V((C // WIDE, R, WIDE), f32), V((R, 128), f32),
            V((R, C), bf16), V((R, C), bf16),
            V((ITERS + 1, G, R // 64, 128), f32), V((ITERS, QUAD, C // 64, 128), f32),
            V((Z, Y, nb, D), f32), V((Z, Y, nb, D), f32), V((Z, nb, D), f32), V((Z, nb, D), f32),
            V((Z, Y, TAIL, D), f32), V((Z, Y, TAIL, D), f32), V((Y, R, 128), f32),
            dma((Z,)), dma((Z,)), dma((Z,)), dma((Z,)),
            dma((Z, Y)), dma((Z, Y)),
            dma((PIECES,)), dma((PIECES,)), dma((2,)), dma((PIECES,)), dma((PIECES,)),
            dma((ITERS + 1, G)), dma((ITERS + 1, G)), dma((ITERS, QUAD)), dma((ITERS, QUAD)),
            dma((Z, HALVES + 1, Y)), dma((Z, HALVES + 1, Y)),
            dma((Z, HALVES + 1)), dma((Z, HALVES + 1)),
            dma((Z, HALVES + 1)), dma((Z, HALVES + 1)), dma((2,)),
        ],
        compiler_params=pltpu.CompilerParams(
            collective_id=0, has_side_effects=True, vmem_limit_bytes=60 * 1024 * 1024),
        cost_estimate=pl.CostEstimate(
            flops=flops, bytes_accessed=8 * (R + C) * D, transcendentals=5 * R * C),
    )(noise, data)


def per_device(Z, Y, noise, data, times):
    targets = targets_of(Z, Y, noise, data)
    path = (1.0 - times)[:, None] * noise + times[:, None] * targets
    return (path, targets - noise)


def solution(mesh):
    Z, Y = mesh.shape["row"], mesh.shape["col"] // QUAD
    in_specs = (P(("row", "col"), None), P(("col", "row"), None), P(("row", "col")))
    out_specs = (P(("row", "col"), None), P(("row", "col"), None))
    return jax.shard_map(
        functools.partial(per_device, Z, Y), mesh=mesh, in_specs=in_specs, out_specs=out_specs,
        check_vma=False,
    )
```

```python
import functools
import math

import jax
import jax.numpy as jnp
from jax import lax
from jax.experimental import pallas as pl
from jax.experimental.pallas import tpu as pltpu
from jax.sharding import PartitionSpec as P

ITERS = 2
EPS = 0.05
PAIR = 2
CORES = 2
QUAD = PAIR * CORES
WIDE = 128 * CORES
PIECES = 4
HALVES = 2
f32 = jnp.float32
bf16 = jnp.bfloat16
NT = (((1,), (1,)), ((), ()))
NN = (((1,), (0,)), ((), ()))


def split(value):
    high = value.astype(bf16)
    return high, (value - high.astype(f32)).astype(bf16)


def dot3(ah, al, bh, bl, dims):
    mm = functools.partial(lax.dot_general, dimension_numbers=dims, preferred_element_type=f32)
    return mm(ah, bh) + (mm(al, bh) + mm(ah, bl))


def dot3_stacked(both, bh, bl, dims):
    mm = functools.partial(lax.dot_general, dimension_numbers=dims, preferred_element_type=f32)
    n = both.shape[0] // 2
    pair = mm(both, bh)
    return pair[:n] + (pair[n:] + mm(both[:n], bl))


def kernel(
    Z, Y, noise_ref, data_ref, out_ref,
    nf, df, nh, nl, dh, dl, rn, cn, score, st, wh, wl, rs, cs, part, yb, ub, db, sc,
    up_s, up_r, dn_s, dn_r, ys, yr, xs, xr, sib, fs, fr, rss, rsr, css, csr,
    ps, pr, us, ur, vs, vr, own,
):
    nb, D = noise_ref.shape
    md = data_ref.shape[0]
    G = Z * Y
    R, C = G * nb, QUAD * md
    mc = md // PIECES
    NB = C // WIDE
    NX = NB // PAIR
    total_noise, total_data = R * QUAD, C * G
    z = lax.axis_index("row")
    col = lax.axis_index("col")
    c = lax.rem(col, CORES)
    x = lax.rem(lax.div(col, CORES), PAIR)
    y = lax.div(col, QUAD)
    g = z * Y + y
    q = x * CORES + c

    def dev(z_, y_, x_, c_):
        return (z_, (y_ * PAIR + x_) * CORES + c_)

    def rc(src, dst, send, recv, device):
        return pltpu.make_async_remote_copy(
            src_ref=src, dst_ref=dst, send_sem=send, recv_sem=recv,
            device_id=device, device_id_type=pl.DeviceIdType.MESH,
        )

    def group_dev(g2):
        return dev(lax.div(g2, Y), lax.rem(g2, Y), x, c)

    def quad_dev(q2):
        return dev(z, y, lax.div(q2, CORES), lax.rem(q2, CORES))

    far, near = jnp.maximum(z, Z - 1 - z), jnp.minimum(z, Z - 1 - z)
    toward = jnp.where(Z - 1 - z >= z, 1, -1)

    def order(n):
        m = n - (far - near)
        late = near - lax.div(jnp.maximum(m, 0), 2)
        flip = jnp.where(lax.rem(jnp.maximum(m, 0), 2) == 0, 1, -1)
        return z + toward * jnp.where(m < 0, far - n, late * flip)

    own_noise = pltpu.make_async_copy(noise_ref, nf.at[g], own.at[0])
    own_data = pltpu.make_async_copy(data_ref, df.at[q], own.at[1])
    own_noise.start()
    own_data.start()

    barrier = pltpu.get_barrier_semaphore()
    for r in range(1, G):
        pl.semaphore_signal(barrier, inc=1, device_id=group_dev(lax.rem(g + r, G)),
                            device_id_type=pl.DeviceIdType.MESH)
    for r in range(1, QUAD):
        pl.semaphore_signal(barrier, inc=1, device_id=quad_dev(lax.rem(q + r, QUAD)),
                            device_id_type=pl.DeviceIdType.MESH)
    pl.semaphore_wait(barrier, G - 1 + QUAD - 1)

    x_dev = dev(z, y, 1 - x, c)
    c_dev = dev(z, y, x, 1 - c)
    qx = (1 - x) * CORES + c
    qc = x * CORES + 1 - c
    qxc = (1 - x) * CORES + 1 - c

    def data_send(k):
        rows = pl.ds(k * mc, mc)
        return rc(data_ref.at[rows], df.at[q, rows], xs.at[k], xr.at[k], x_dev)

    def data_recv(k):
        rows = pl.ds(k * mc, mc)
        return rc(data_ref.at[rows], df.at[qx, rows], xs.at[k], xr.at[k], x_dev)

    def data_forward(k):
        rows = pl.ds(k * mc, mc)
        return rc(df.at[qx, rows], df.at[qx, rows], fs.at[k], fr.at[k], c_dev)

    def data_forwarded(k):
        rows = pl.ds(k * mc, mc)
        return rc(df.at[qxc, rows], df.at[qxc, rows], fs.at[k], fr.at[k], c_dev)

    def up_copy(zz, s):
        slot = nf.at[zz * Y + y]
        return rc(slot, slot, up_s.at[s], up_r.at[s], dev(z + 1, y, x, c))

    def dn_copy(zz, s):
        slot = nf.at[zz * Y + y]
        return rc(slot, slot, dn_s.at[s], dn_r.at[s], dev(z - 1, y, x, c))

    def y_copy(zz, r):
        slot = nf.at[zz * Y + y]
        return rc(slot, slot, ys.at[zz, r], yr.at[zz, y], dev(z, lax.rem(y + r, Y), x, c))

    def y_landed(zz, r):
        y2 = lax.rem(y + r, Y)
        slot = nf.at[zz * Y + y2]
        return rc(slot, slot, ys.at[zz, r], yr.at[zz, y2], dev(z, y2, x, c))

    def y_sends(zz):
        for r in range(1, Y):
            y_copy(zz, r).start()

    for k in range(PIECES - 1):
        data_send(k).start()
    sib_copy = rc(data_ref, df.at[q], sib.at[0], sib.at[1], c_dev)
    sib_copy.start()
    own_noise.wait()
    y_sends(z)
    pl.when(z + 1 < Z)(lambda: up_copy(z, 0).start())
    pl.when(z > 0)(lambda: dn_copy(z, 0).start())
    def convert(src, slot, base, at, count, high, low, norm):
        step = min(32, count)

        def body(i, carry):
            value = src[slot, pl.ds(pl.multiple_of(base + i * step, step), step), :]
            rows = pl.ds(pl.multiple_of(at + i * step, step), step)
            h, l = split(value)
            high[rows, :] = h
            low[rows, :] = l
            norm[rows, :] = jnp.broadcast_to(
                jnp.sum(value * value, axis=1, keepdims=True), (step, 128))
            return carry

        lax.fori_loop(0, count // step, body, 0)

    def convert_noise(slot):
        convert(nf, slot, 0, slot * nb, nb, nh, nl, rn)

    def convert_data(slot, k, count):
        step = min(count, 128)
        for base in range(k * mc, k * mc + count, step):
            at = (lax.div(slot, CORES) * (NX * WIDE) + lax.rem(slot, CORES) * 128
                  + base // 128 * WIDE + base % 128)
            convert(df, slot, base, at, step, dh, dl, cn)

    convert_noise(g)
    own_data.wait()
    convert_data(q, 0, md)
    rc(data_ref, df.at[qc], sib.at[0], sib.at[1], c_dev).wait_recv()
    convert_data(qc, 0, md)

    def score_finish(cross, at, count, j):
        rows, cols = pl.ds(at, count), pl.ds(pl.multiple_of(j * WIDE, WIDE), WIDE)
        norms = cn[cols, :].T[0:1, :]
        for t in range(WIDE // 128):
            lanes = slice(t * 128, (t + 1) * 128)
            score[j, rows, lanes] = (
                2.0 * cross[:, lanes] - rn[rows, :] - norms[:, lanes]) * (1.0 / (D * EPS))

    def score_pair(zz, j):
        at, count = pl.multiple_of(zz * (Y * nb), Y * nb), Y * nb
        rows, cols = pl.ds(at, count), pl.ds(pl.multiple_of(j * WIDE, WIDE), WIDE)
        both = jnp.concatenate([nh[rows, :], nl[rows, :]], axis=0)
        score_finish(dot3_stacked(both, dh[cols, :], dl[cols, :], NT), at, count, j)

    def y_arrivals(zz):
        for r in range(1, Y):
            y_landed(zz, r).wait_recv()
            convert_noise(zz * Y + lax.rem(y + r, Y))

        def body(i, carry):
            score_pair(zz, x * NX + i)
            return carry

        lax.fori_loop(0, NX, body, 0)

    def data_piece(k):
        data_recv(k).wait_recv()
        data_forward(k).start()

    def data_piece_forwarded(k):
        data_forwarded(k).wait_recv()
        convert_data(qxc, k, mc)

    for s in range(1, Z):
        lo, hi = z - s, z + s

        @pl.when(lo >= 0)
        def _():
            up_copy(lo, s - 1).wait_recv()
            if s < Z - 1:
                pl.when(z + 1 < Z)(lambda: up_copy(lo, s).start())
            y_sends(lo)

        @pl.when(hi < Z)
        def _():
            dn_copy(hi, s - 1).wait_recv()
            if s < Z - 1:
                pl.when(z > 0)(lambda: dn_copy(hi, s).start())
            y_sends(hi)

        if s == min(2, Z - 1):
            data_send(PIECES - 1).start()
        pl.when(lo >= 0)(lambda: convert_noise(lo * Y + y))
        pl.when(hi < Z)(lambda: convert_noise(hi * Y + y))
        if s == Z - 1:
            for k in range(PIECES // 2):
                data_piece(k)
                convert_data(qx, k, mc)
            for k in range(PIECES // 2):
                data_piece_forwarded(k)
        if s == 1:
            pl.when(z != order(0))(lambda: y_arrivals(z))
        else:
            pl.when((lo + 1 >= 0) & (lo + 1 != order(0)))(lambda: y_arrivals(lo + 1))
            pl.when((hi - 1 < Z) & (hi - 1 != order(0)))(lambda: y_arrivals(hi - 1))

    def early_body(n, carry):
        for i in range(NX - 1):
            score_pair(order(n), (1 - x) * NX + i)
        return carry

    lax.fori_loop(1, Z, early_body, 0)
    for k in range(PIECES // 2, PIECES):
        data_piece(k)
        if k < PIECES - 1:
            convert_data(qx, k, mc)
    y_arrivals(order(0))
    early_body(0, 0)
    convert_data(qx, PIECES - 1, mc)
    for k in range(PIECES // 2, PIECES):
        data_piece_forwarded(k)

    last = (1 - x) * NX + NX - 1
    cols = pl.ds(pl.multiple_of(last * WIDE, WIDE), WIDE)
    score_finish(dot3(nh[...], nl[...], dh[cols, :], dl[cols, :], NT), 0, R, last)

    lane = lax.broadcasted_iota(jnp.int32, (1, 128), 1)
    RB, CB, SB = R // 128, C // 128, WIDE // 128
    block = Y * nb

    def row_block(pot, weights, i):
        def shift(j):
            return jnp.concatenate([pot[j * SB + t:j * SB + t + 1] for t in range(SB)], axis=1)

        rows = pl.ds(pl.multiple_of(i * block, block), block)
        vals = [score[j, rows, :] + (0.0 if pot is None else shift(j))
                for j in range(NB)]
        peak = functools.reduce(jnp.maximum, vals)
        peak = jnp.max(peak, axis=1, keepdims=True)
        exps = [jnp.exp(v - peak) for v in vals]
        total = jnp.sum(functools.reduce(jnp.add, exps), axis=1, keepdims=True)
        st[rows, :] = jnp.where(lane == 0, peak, total)
        if weights:
            for j in range(NB):
                h, l = split(exps[j])
                wh[rows, j * WIDE:(j + 1) * WIDE] = h
                wl[rows, j * WIDE:(j + 1) * WIDE] = l

    def row_pass(pot):
        def body(i, carry):
            row_block(pot, False, i)
            return carry

        lax.fori_loop(0, Z, body, 0)

    def row_copy(ex, r, landed=False):
        g2 = lax.rem(g + r, G)
        at = g2 if landed else g
        return rc(rs.at[ex, at], rs.at[ex, at], rss.at[ex, r], rsr.at[ex, at], group_dev(g2))

    def row_exchange(ex):
        for k in range(RB):
            turned = st[k * 128:(k + 1) * 128, :].T
            rs[ex, g, k:k + 1, :] = turned[0:1]
            rs[ex, g, RB + k:RB + k + 1, :] = turned[1:2]
        for r in range(1, G):
            row_copy(ex, r).start()

    def row_combine(ex):
        for r in range(1, G):
            row_copy(ex, r, True).wait_recv()
        peaks = [rs[ex, k, 0:RB, :] for k in range(G)]
        top = functools.reduce(jnp.maximum, peaks)
        total = sum(rs[ex, k, RB:2 * RB, :] * jnp.exp(peaks[k] - top) for k in range(G))
        return top, total

    def col_copy(ex, r, landed=False):
        q2 = lax.rem(q + r, QUAD)
        at = q2 if landed else q
        return rc(cs.at[ex, at], cs.at[ex, at], css.at[ex, r], csr.at[ex, at], quad_dev(q2))

    def spread(ref, packed):
        for k in range(RB):
            ref[k * 128:(k + 1) * 128, :] = jnp.broadcast_to(packed[k:k + 1], (128, 128)).T

    pot = None
    for step in range(ITERS):
        row_pass(pot)
        row_exchange(step)
        top, total = row_combine(step)
        spread(st, math.log(total_data) - (top + jnp.log(total)))
        for j in range(NB):
            for t in range(SB):
                lanes, at = slice(t * 128, (t + 1) * 128), j * SB + t
                val = score[j, :, lanes] + st[...]
                peak = jnp.max(val, axis=0, keepdims=True)
                total = jnp.sum(jnp.exp(val - peak), axis=0, keepdims=True)
                cs[step, q, at:at + 1, :] = peak
                cs[step, q, CB + at:CB + at + 1, :] = total
        for r in range(1, QUAD):
            col_copy(step, r).start()
        for r in range(1, QUAD):
            col_copy(step, r, True).wait_recv()
        peaks = [cs[step, k, 0:CB, :] for k in range(QUAD)]
        top = functools.reduce(jnp.maximum, peaks)
        total = sum(cs[step, k, CB:2 * CB, :] * jnp.exp(peaks[k] - top) for k in range(QUAD))
        pot = math.log(total_noise) - (top + jnp.log(total))

    cutat = -(-nb // (8 * HALVES)) * 8
    pieces = [pl.ds(h * cutat, min(cutat, nb - h * cutat)) for h in range(HALVES)]

    def part_copy(zz, h, r, landed=False):
        y2 = lax.rem(y + r, Y)
        rows, at = pieces[h], y2 if landed else y
        return rc(part.at[zz, y2, rows], yb.at[zz, at, rows],
                  ps.at[zz, h, r], pr.at[zz, h, at], dev(z, y2, x, c))

    def up_part(zz, h):
        return rc(part.at[zz, y, pieces[h]], ub.at[zz, pieces[h]], us.at[zz, h], ur.at[zz, h],
                  dev(z + 1, y, x, c))

    def dn_part(zz, h):
        return rc(part.at[zz, y, pieces[h]], db.at[zz, pieces[h]], vs.at[zz, h], vr.at[zz, h],
                  dev(z - 1, y, x, c))

    def multiply(zz):
        rows = pl.ds(pl.multiple_of(zz * (Y * nb), Y * nb), Y * nb)
        both = jnp.concatenate([wh[rows, :], wl[rows, :]], axis=0)
        for n in range(D // 256):
            lanes = slice(n * 256, (n + 1) * 256)
            numer = dot3_stacked(both, dh[:, lanes], dl[:, lanes], NN)
            for t in range(2):
                piece = numer[:, t * 128:(t + 1) * 128]
                for k in range(Y):
                    part[zz, k, :, n * 256 + t * 128:n * 256 + (t + 1) * 128] = (
                        piece[k * nb:(k + 1) * nb])

    def launch(zz):
        for h in range(HALVES):
            for r in range(1, Y):
                part_copy(zz, h, r).start()

    def weigh(n, carry):
        row_block(pot, True, order(n))
        return carry

    first = order(jnp.int32(0))
    weigh(jnp.int32(0), 0)
    multiply(first)
    launch(first)
    lax.fori_loop(1, Z, weigh, 0)
    row_exchange(ITERS)

    def multiply_body(n, carry):
        multiply(order(n))
        launch(order(n))
        return carry

    lax.fori_loop(1, Z, multiply_body, 0)
    top, total = row_combine(ITERS)
    for k in range(Y):
        spread(sc.at[k], jnp.exp(rs[ITERS, z * Y + k, 0:RB, :] - top) / total)

    for k in range(PIECES):
        data_send(k).wait_send()
        data_forward(k).wait_send()
    sib_copy.wait_send()
    for s in range(Z - 1):
        pl.when((z - s >= 0) & (z + 1 < Z))(lambda: up_copy(z - s, s).wait_send())
        pl.when((z + s < Z) & (z > 0))(lambda: dn_copy(z + s, s).wait_send())
    for ex in range(ITERS + 1):
        for r in range(1, G):
            row_copy(ex, r).wait_send()
    for ex in range(ITERS):
        for r in range(1, QUAD):
            col_copy(ex, r).wait_send()
    for zz in range(Z):
        for r in range(1, Y):
            y_copy(zz, r).wait_send()

    def reduce_body(n, carry):
        zz = order(n)
        for h, rows in enumerate(pieces):
            for r in range(1, Y):
                part_copy(zz, h, r, True).wait_recv()
            base = pl.multiple_of(zz * (Y * nb) + y * nb + rows.start, 8)
            scales = [sc[lax.rem(y + r, Y), pl.ds(base, rows.size), :] for r in range(Y)]
            for t in range(D // 128):
                lanes = slice(t * 128, (t + 1) * 128)
                value = part[zz, y, rows, lanes] * scales[0]
                for r in range(1, Y):
                    value += yb[zz, lax.rem(y + r, Y), rows, lanes] * scales[r]
                part[zz, y, rows, lanes] = value

            @pl.when((zz >= z) & (z > 0))
            def _():
                up_part(zz, h).wait_recv()
                part[zz, y, rows, :] += ub[zz, rows, :]

            @pl.when((zz <= z) & (z + 1 < Z))
            def _():
                dn_part(zz, h).wait_recv()
                part[zz, y, rows, :] += db[zz, rows, :]

            pl.when(zz > z)(lambda: up_part(zz, h).start())
            pl.when(zz < z)(lambda: dn_part(zz, h).start())
        return carry

    lax.fori_loop(0, Z, reduce_body, 0)
    out_ref[...] = part[z, y]

    for zz in range(Z):
        for h in range(HALVES):
            for r in range(1, Y):
                part_copy(zz, h, r).wait_send()
            pl.when(zz > z)(lambda: up_part(zz, h).wait_send())
            pl.when(zz < z)(lambda: dn_part(zz, h).wait_send())


def targets_of(Z, Y, noise, data):
    nb, D = noise.shape
    md = data.shape[0]
    G = Z * Y
    R, C = G * nb, QUAD * md
    V, dma = pltpu.VMEM, pltpu.SemaphoreType.DMA
    flops = 2 * 6 * R * C * D
    return pl.pallas_call(
        functools.partial(kernel, Z, Y),
        out_shape=jax.ShapeDtypeStruct((nb, D), f32),
        in_specs=[pl.BlockSpec(memory_space=pl.ANY)] * 2,
        out_specs=pl.BlockSpec(memory_space=pltpu.VMEM),
        scratch_shapes=[
            V((G, nb, D), f32), V((QUAD, md, D), f32),
            V((R, D), bf16), V((R, D), bf16), V((C, D), bf16), V((C, D), bf16),
            V((R, 128), f32), V((C, 128), f32),
            V((C // WIDE, R, WIDE), f32), V((R, 128), f32),
            V((R, C), bf16), V((R, C), bf16),
            V((ITERS + 1, G, R // 64, 128), f32), V((ITERS, QUAD, C // 64, 128), f32),
            V((Z, Y, nb, D), f32), V((Z, Y, nb, D), f32), V((Z, nb, D), f32), V((Z, nb, D), f32),
            V((Y, R, 128), f32),
            dma((Z,)), dma((Z,)), dma((Z,)), dma((Z,)),
            dma((Z, Y)), dma((Z, Y)),
            dma((PIECES,)), dma((PIECES,)), dma((2,)), dma((PIECES,)), dma((PIECES,)),
            dma((ITERS + 1, G)), dma((ITERS + 1, G)), dma((ITERS, QUAD)), dma((ITERS, QUAD)),
            dma((Z, HALVES, Y)), dma((Z, HALVES, Y)),
            dma((Z, HALVES)), dma((Z, HALVES)),
            dma((Z, HALVES)), dma((Z, HALVES)), dma((2,)),
        ],
        compiler_params=pltpu.CompilerParams(
            collective_id=0, has_side_effects=True, vmem_limit_bytes=60 * 1024 * 1024),
        cost_estimate=pl.CostEstimate(
            flops=flops, bytes_accessed=8 * (R + C) * D, transcendentals=5 * R * C),
    )(noise, data)


def per_device(Z, Y, noise, data, times):
    targets = targets_of(Z, Y, noise, data)
    path = (1.0 - times)[:, None] * noise + times[:, None] * targets
    return (path, targets - noise)


def solution(mesh):
    Z, Y = mesh.shape["row"], mesh.shape["col"] // QUAD
    in_specs = (P(("row", "col"), None), P(("col", "row"), None), P(("row", "col")))
    out_specs = (P(("row", "col"), None), P(("row", "col"), None))
    return jax.shard_map(
        functools.partial(per_device, Z, Y), mesh=mesh, in_specs=in_specs, out_specs=out_specs,
        check_vma=False,
    )
```

```python
import functools
import math

import jax
import jax.numpy as jnp
from jax import lax
from jax.experimental import pallas as pl
from jax.experimental.pallas import tpu as pltpu
from jax.sharding import PartitionSpec as P

ITERS = 2
EPS = 0.05
PAIR = 2
CORES = 2
QUAD = PAIR * CORES
WIDE = 128 * CORES
PIECES = 4
HALVES = 2
f32 = jnp.float32
bf16 = jnp.bfloat16
NT = (((1,), (1,)), ((), ()))
NN = (((1,), (0,)), ((), ()))


def split(value):
    high = value.astype(bf16)
    return high, (value - high.astype(f32)).astype(bf16)


def dot3(ah, al, bh, bl, dims):
    mm = functools.partial(lax.dot_general, dimension_numbers=dims, preferred_element_type=f32)
    return mm(ah, bh) + (mm(al, bh) + mm(ah, bl))


def dot3_stacked(both, bh, bl, dims):
    mm = functools.partial(lax.dot_general, dimension_numbers=dims, preferred_element_type=f32)
    n = both.shape[0] // 2
    pair = mm(both, bh)
    return pair[:n] + (pair[n:] + mm(both[:n], bl))


def kernel(
    Z, Y, noise_ref, data_ref, out_ref,
    nf, df, nh, nl, dh, dl, rn, cn, score, st, wh, wl, rs, cs, part, yb, ub, db, sc,
    up_s, up_r, dn_s, dn_r, ys, yr, xs, xr, sib, fs, fr, rss, rsr, css, csr,
    ps, pr, us, ur, vs, vr, own,
):
    nb, D = noise_ref.shape
    md = data_ref.shape[0]
    G = Z * Y
    R, C = G * nb, QUAD * md
    mc = md // PIECES
    NB = C // WIDE
    NX = NB // PAIR
    total_noise, total_data = R * QUAD, C * G
    z = lax.axis_index("row")
    col = lax.axis_index("col")
    c = lax.rem(col, CORES)
    x = lax.rem(lax.div(col, CORES), PAIR)
    y = lax.div(col, QUAD)
    g = z * Y + y
    q = x * CORES + c

    def dev(z_, y_, x_, c_):
        return (z_, (y_ * PAIR + x_) * CORES + c_)

    def rc(src, dst, send, recv, device):
        return pltpu.make_async_remote_copy(
            src_ref=src, dst_ref=dst, send_sem=send, recv_sem=recv,
            device_id=device, device_id_type=pl.DeviceIdType.MESH,
        )

    def group_dev(g2):
        return dev(lax.div(g2, Y), lax.rem(g2, Y), x, c)

    def quad_dev(q2):
        return dev(z, y, lax.div(q2, CORES), lax.rem(q2, CORES))

    far, near = jnp.maximum(z, Z - 1 - z), jnp.minimum(z, Z - 1 - z)
    toward = jnp.where(Z - 1 - z >= z, 1, -1)

    def order(n):
        m = n - (far - near)
        late = near - lax.div(jnp.maximum(m, 0), 2)
        flip = jnp.where(lax.rem(jnp.maximum(m, 0), 2) == 0, 1, -1)
        return z + toward * jnp.where(m < 0, far - n, late * flip)

    own_noise = pltpu.make_async_copy(noise_ref, nf.at[g], own.at[0])
    own_data = pltpu.make_async_copy(data_ref, df.at[q], own.at[1])
    own_noise.start()
    own_data.start()

    barrier = pltpu.get_barrier_semaphore()
    for r in range(1, G):
        pl.semaphore_signal(barrier, inc=1, device_id=group_dev(lax.rem(g + r, G)),
                            device_id_type=pl.DeviceIdType.MESH)
    for r in range(1, QUAD):
        pl.semaphore_signal(barrier, inc=1, device_id=quad_dev(lax.rem(q + r, QUAD)),
                            device_id_type=pl.DeviceIdType.MESH)
    pl.semaphore_wait(barrier, G - 1 + QUAD - 1)

    x_dev = dev(z, y, 1 - x, c)
    c_dev = dev(z, y, x, 1 - c)
    qx = (1 - x) * CORES + c
    qc = x * CORES + 1 - c
    qxc = (1 - x) * CORES + 1 - c

    def data_send(k):
        rows = pl.ds(k * mc, mc)
        return rc(data_ref.at[rows], df.at[q, rows], xs.at[k], xr.at[k], x_dev)

    def data_recv(k):
        rows = pl.ds(k * mc, mc)
        return rc(data_ref.at[rows], df.at[qx, rows], xs.at[k], xr.at[k], x_dev)

    def data_forward(k):
        rows = pl.ds(k * mc, mc)
        return rc(df.at[qx, rows], df.at[qx, rows], fs.at[k], fr.at[k], c_dev)

    def data_forwarded(k):
        rows = pl.ds(k * mc, mc)
        return rc(df.at[qxc, rows], df.at[qxc, rows], fs.at[k], fr.at[k], c_dev)

    def up_copy(zz, s):
        slot = nf.at[zz * Y + y]
        return rc(slot, slot, up_s.at[s], up_r.at[s], dev(z + 1, y, x, c))

    def dn_copy(zz, s):
        slot = nf.at[zz * Y + y]
        return rc(slot, slot, dn_s.at[s], dn_r.at[s], dev(z - 1, y, x, c))

    def y_copy(zz, r):
        slot = nf.at[zz * Y + y]
        return rc(slot, slot, ys.at[zz, r], yr.at[zz, y], dev(z, lax.rem(y + r, Y), x, c))

    def y_landed(zz, r):
        y2 = lax.rem(y + r, Y)
        slot = nf.at[zz * Y + y2]
        return rc(slot, slot, ys.at[zz, r], yr.at[zz, y2], dev(z, y2, x, c))

    def y_sends(zz):
        for r in range(1, Y):
            y_copy(zz, r).start()

    for k in range(PIECES - 1):
        data_send(k).start()
    sib_copy = rc(data_ref, df.at[q], sib.at[0], sib.at[1], c_dev)
    sib_copy.start()
    own_noise.wait()
    y_sends(z)
    pl.when(z + 1 < Z)(lambda: up_copy(z, 0).start())
    pl.when(z > 0)(lambda: dn_copy(z, 0).start())
    def convert(src, slot, base, at, count, high, low, norm):
        step = min(32, count)

        def body(i, carry):
            value = src[slot, pl.ds(pl.multiple_of(base + i * step, step), step), :]
            rows = pl.ds(pl.multiple_of(at + i * step, step), step)
            h, l = split(value)
            high[rows, :] = h
            low[rows, :] = l
            norm[rows, :] = jnp.broadcast_to(
                jnp.sum(value * value, axis=1, keepdims=True), (step, 128))
            return carry

        lax.fori_loop(0, count // step, body, 0)

    def convert_noise(slot):
        convert(nf, slot, 0, slot * nb, nb, nh, nl, rn)

    def convert_data(slot, k, count):
        step = min(count, 128)
        for base in range(k * mc, k * mc + count, step):
            at = (lax.div(slot, CORES) * (NX * WIDE) + lax.rem(slot, CORES) * 128
                  + base // 128 * WIDE + base % 128)
            convert(df, slot, base, at, step, dh, dl, cn)

    convert_noise(g)
    own_data.wait()
    convert_data(q, 0, md)
    rc(data_ref, df.at[qc], sib.at[0], sib.at[1], c_dev).wait_recv()
    convert_data(qc, 0, md)

    def score_finish(cross, at, count, j):
        rows, cols = pl.ds(at, count), pl.ds(pl.multiple_of(j * WIDE, WIDE), WIDE)
        norms = cn[cols, :].T[0:1, :]
        for t in range(WIDE // 128):
            lanes = slice(t * 128, (t + 1) * 128)
            score[j, rows, lanes] = (
                2.0 * cross[:, lanes] - rn[rows, :] - norms[:, lanes]) * (1.0 / (D * EPS))

    def score_pair(zz, j):
        at, count = pl.multiple_of(zz * (Y * nb), Y * nb), Y * nb
        rows, cols = pl.ds(at, count), pl.ds(pl.multiple_of(j * WIDE, WIDE), WIDE)
        both = jnp.concatenate([nh[rows, :], nl[rows, :]], axis=0)
        score_finish(dot3_stacked(both, dh[cols, :], dl[cols, :], NT), at, count, j)

    def y_arrivals(zz):
        for r in range(1, Y):
            y_landed(zz, r).wait_recv()
            convert_noise(zz * Y + lax.rem(y + r, Y))

        def body(i, carry):
            score_pair(zz, x * NX + i)
            return carry

        lax.fori_loop(0, NX, body, 0)

    def data_piece(k):
        data_recv(k).wait_recv()
        data_forward(k).start()

    def data_piece_forwarded(k):
        data_forwarded(k).wait_recv()
        convert_data(qxc, k, mc)

    for s in range(1, Z):
        lo, hi = z - s, z + s

        @pl.when(lo >= 0)
        def _():
            up_copy(lo, s - 1).wait_recv()
            if s < Z - 1:
                pl.when(z + 1 < Z)(lambda: up_copy(lo, s).start())
            y_sends(lo)

        @pl.when(hi < Z)
        def _():
            dn_copy(hi, s - 1).wait_recv()
            if s < Z - 1:
                pl.when(z > 0)(lambda: dn_copy(hi, s).start())
            y_sends(hi)

        if s == min(2, Z - 1):
            data_send(PIECES - 1).start()
        pl.when(lo >= 0)(lambda: convert_noise(lo * Y + y))
        pl.when(hi < Z)(lambda: convert_noise(hi * Y + y))
        if s == Z - 1:
            for k in range(PIECES // 2):
                data_piece(k)
                convert_data(qx, k, mc)
            for k in range(PIECES // 2):
                data_piece_forwarded(k)
        if s == 1:
            pl.when(z != order(0))(lambda: y_arrivals(z))
        else:
            pl.when((lo + 1 >= 0) & (lo + 1 != order(0)))(lambda: y_arrivals(lo + 1))
            pl.when((hi - 1 < Z) & (hi - 1 != order(0)))(lambda: y_arrivals(hi - 1))

    def early_body(n, carry):
        for i in range(NX - 1):
            score_pair(order(n), (1 - x) * NX + i)
        return carry

    lax.fori_loop(1, Z, early_body, 0)
    for k in range(PIECES // 2, PIECES):
        data_piece(k)
        if k < PIECES - 1:
            convert_data(qx, k, mc)
    y_arrivals(order(0))
    early_body(0, 0)
    convert_data(qx, PIECES - 1, mc)
    for k in range(PIECES // 2, PIECES):
        data_piece_forwarded(k)

    last = (1 - x) * NX + NX - 1
    cols = pl.ds(pl.multiple_of(last * WIDE, WIDE), WIDE)
    score_finish(dot3(nh[...], nl[...], dh[cols, :], dl[cols, :], NT), 0, R, last)

    lane = lax.broadcasted_iota(jnp.int32, (1, 128), 1)
    RB, CB, SB = R // 128, C // 128, WIDE // 128
    block = Y * nb

    def row_block(pot, weights, i):
        def shift(j):
            return jnp.concatenate([pot[j * SB + t:j * SB + t + 1] for t in range(SB)], axis=1)

        rows = pl.ds(pl.multiple_of(i * block, block), block)
        vals = [score[j, rows, :] + (0.0 if pot is None else shift(j))
                for j in range(NB)]
        peak = functools.reduce(jnp.maximum, vals)
        peak = jnp.max(peak, axis=1, keepdims=True)
        exps = [jnp.exp(v - peak) for v in vals]
        total = jnp.sum(functools.reduce(jnp.add, exps), axis=1, keepdims=True)
        st[rows, :] = jnp.where(lane == 0, peak, total)
        if weights:
            for j in range(NB):
                h, l = split(exps[j])
                wh[rows, j * WIDE:(j + 1) * WIDE] = h
                wl[rows, j * WIDE:(j + 1) * WIDE] = l

    def row_pass(pot):
        def body(i, carry):
            row_block(pot, False, i)
            return carry

        lax.fori_loop(0, Z, body, 0)

    def row_copy(ex, r, landed=False):
        g2 = lax.rem(g + r, G)
        at = g2 if landed else g
        return rc(rs.at[ex, at], rs.at[ex, at], rss.at[ex, r], rsr.at[ex, at], group_dev(g2))

    def row_exchange(ex):
        for k in range(RB):
            turned = st[k * 128:(k + 1) * 128, :].T
            rs[ex, g, k:k + 1, :] = turned[0:1]
            rs[ex, g, RB + k:RB + k + 1, :] = turned[1:2]
        for r in range(1, G):
            row_copy(ex, r).start()

    def row_combine(ex):
        for r in range(1, G):
            row_copy(ex, r, True).wait_recv()
        peaks = [rs[ex, k, 0:RB, :] for k in range(G)]
        top = functools.reduce(jnp.maximum, peaks)
        total = sum(rs[ex, k, RB:2 * RB, :] * jnp.exp(peaks[k] - top) for k in range(G))
        return top, total

    def col_copy(ex, r, landed=False):
        q2 = lax.rem(q + r, QUAD)
        at = q2 if landed else q
        return rc(cs.at[ex, at], cs.at[ex, at], css.at[ex, r], csr.at[ex, at], quad_dev(q2))

    def spread(ref, packed):
        for k in range(RB):
            ref[k * 128:(k + 1) * 128, :] = jnp.broadcast_to(packed[k:k + 1], (128, 128)).T

    pot = None
    for step in range(ITERS):
        row_pass(pot)
        row_exchange(step)
        top, total = row_combine(step)
        spread(st, math.log(total_data) - (top + jnp.log(total)))
        for j in range(NB):
            for t in range(SB):
                lanes, at = slice(t * 128, (t + 1) * 128), j * SB + t
                val = score[j, :, lanes] + st[...]
                peak = jnp.max(val, axis=0, keepdims=True)
                total = jnp.sum(jnp.exp(val - peak), axis=0, keepdims=True)
                cs[step, q, at:at + 1, :] = peak
                cs[step, q, CB + at:CB + at + 1, :] = total
        for r in range(1, QUAD):
            col_copy(step, r).start()
        for r in range(1, QUAD):
            col_copy(step, r, True).wait_recv()
        peaks = [cs[step, k, 0:CB, :] for k in range(QUAD)]
        top = functools.reduce(jnp.maximum, peaks)
        total = sum(cs[step, k, CB:2 * CB, :] * jnp.exp(peaks[k] - top) for k in range(QUAD))
        pot = math.log(total_noise) - (top + jnp.log(total))

    cutat = -(-nb // (8 * HALVES)) * 8
    pieces = [pl.ds(h * cutat, min(cutat, nb - h * cutat)) for h in range(HALVES)]

    def part_copy(zz, h, r, landed=False):
        y2 = lax.rem(y + r, Y)
        rows, at = pieces[h], y2 if landed else y
        return rc(part.at[zz, y2, rows], yb.at[zz, at, rows],
                  ps.at[zz, h, r], pr.at[zz, h, at], dev(z, y2, x, c))

    def up_part(zz, h):
        return rc(part.at[zz, y, pieces[h]], ub.at[zz, pieces[h]], us.at[zz, h], ur.at[zz, h],
                  dev(z + 1, y, x, c))

    def dn_part(zz, h):
        return rc(part.at[zz, y, pieces[h]], db.at[zz, pieces[h]], vs.at[zz, h], vr.at[zz, h],
                  dev(z - 1, y, x, c))

    def multiply(zz):
        rows = pl.ds(pl.multiple_of(zz * (Y * nb), Y * nb), Y * nb)
        both = jnp.concatenate([wh[rows, :], wl[rows, :]], axis=0)
        for n in range(D // 256):
            lanes = slice(n * 256, (n + 1) * 256)
            numer = dot3_stacked(both, dh[:, lanes], dl[:, lanes], NN)
            for t in range(2):
                piece = numer[:, t * 128:(t + 1) * 128]
                for k in range(Y):
                    part[zz, k, :, n * 256 + t * 128:n * 256 + (t + 1) * 128] = (
                        piece[k * nb:(k + 1) * nb])

    def launch(zz):
        for h in range(HALVES):
            for r in range(1, Y):
                part_copy(zz, h, r).start()

    def weigh(n, carry):
        row_block(pot, True, order(n))
        return carry

    first = order(jnp.int32(0))
    weigh(jnp.int32(0), 0)
    multiply(first)
    launch(first)
    lax.fori_loop(1, Z, weigh, 0)
    row_exchange(ITERS)

    def multiply_body(n, carry):
        multiply(order(n))
        return carry

    lax.fori_loop(1, Z, multiply_body, 0)
    top, total = row_combine(ITERS)
    for k in range(Y):
        spread(sc.at[k], jnp.exp(rs[ITERS, z * Y + k, 0:RB, :] - top) / total)

    for k in range(PIECES):
        data_send(k).wait_send()
        data_forward(k).wait_send()
    sib_copy.wait_send()
    for s in range(Z - 1):
        pl.when((z - s >= 0) & (z + 1 < Z))(lambda: up_copy(z - s, s).wait_send())
        pl.when((z + s < Z) & (z > 0))(lambda: dn_copy(z + s, s).wait_send())
    for ex in range(ITERS + 1):
        for r in range(1, G):
            row_copy(ex, r).wait_send()
    for ex in range(ITERS):
        for r in range(1, QUAD):
            col_copy(ex, r).wait_send()
    for zz in range(Z):
        for r in range(1, Y):
            y_copy(zz, r).wait_send()

    def reduce_body(n, carry):
        zz = order(n)
        for h, rows in enumerate(pieces):
            for r in range(1, Y):
                part_copy(zz, h, r, True).wait_recv()

            @pl.when(n + 1 < Z)
            def _():
                for r in range(1, Y):
                    part_copy(order(n + 1), h, r).start()

            base = pl.multiple_of(zz * (Y * nb) + y * nb + rows.start, 8)
            scales = [sc[lax.rem(y + r, Y), pl.ds(base, rows.size), :] for r in range(Y)]
            for t in range(D // 128):
                lanes = slice(t * 128, (t + 1) * 128)
                value = part[zz, y, rows, lanes] * scales[0]
                for r in range(1, Y):
                    value += yb[zz, lax.rem(y + r, Y), rows, lanes] * scales[r]
                part[zz, y, rows, lanes] = value

            @pl.when((zz >= z) & (z > 0))
            def _():
                up_part(zz, h).wait_recv()
                part[zz, y, rows, :] += ub[zz, rows, :]

            @pl.when((zz <= z) & (z + 1 < Z))
            def _():
                dn_part(zz, h).wait_recv()
                part[zz, y, rows, :] += db[zz, rows, :]

            pl.when(zz > z)(lambda: up_part(zz, h).start())
            pl.when(zz < z)(lambda: dn_part(zz, h).start())
        return carry

    lax.fori_loop(0, Z, reduce_body, 0)
    out_ref[...] = part[z, y]

    for zz in range(Z):
        for h in range(HALVES):
            for r in range(1, Y):
                part_copy(zz, h, r).wait_send()
            pl.when(zz > z)(lambda: up_part(zz, h).wait_send())
            pl.when(zz < z)(lambda: dn_part(zz, h).wait_send())


def targets_of(Z, Y, noise, data):
    nb, D = noise.shape
    md = data.shape[0]
    G = Z * Y
    R, C = G * nb, QUAD * md
    V, dma = pltpu.VMEM, pltpu.SemaphoreType.DMA
    flops = 2 * 6 * R * C * D
    return pl.pallas_call(
        functools.partial(kernel, Z, Y),
        out_shape=jax.ShapeDtypeStruct((nb, D), f32),
        in_specs=[pl.BlockSpec(memory_space=pl.ANY)] * 2,
        out_specs=pl.BlockSpec(memory_space=pltpu.VMEM),
        scratch_shapes=[
            V((G, nb, D), f32), V((QUAD, md, D), f32),
            V((R, D), bf16), V((R, D), bf16), V((C, D), bf16), V((C, D), bf16),
            V((R, 128), f32), V((C, 128), f32),
            V((C // WIDE, R, WIDE), f32), V((R, 128), f32),
            V((R, C), bf16), V((R, C), bf16),
            V((ITERS + 1, G, R // 64, 128), f32), V((ITERS, QUAD, C // 64, 128), f32),
            V((Z, Y, nb, D), f32), V((Z, Y, nb, D), f32), V((Z, nb, D), f32), V((Z, nb, D), f32),
            V((Y, R, 128), f32),
            dma((Z,)), dma((Z,)), dma((Z,)), dma((Z,)),
            dma((Z, Y)), dma((Z, Y)),
            dma((PIECES,)), dma((PIECES,)), dma((2,)), dma((PIECES,)), dma((PIECES,)),
            dma((ITERS + 1, G)), dma((ITERS + 1, G)), dma((ITERS, QUAD)), dma((ITERS, QUAD)),
            dma((Z, HALVES, Y)), dma((Z, HALVES, Y)),
            dma((Z, HALVES)), dma((Z, HALVES)),
            dma((Z, HALVES)), dma((Z, HALVES)), dma((2,)),
        ],
        compiler_params=pltpu.CompilerParams(
            collective_id=0, has_side_effects=True, vmem_limit_bytes=60 * 1024 * 1024),
        cost_estimate=pl.CostEstimate(
            flops=flops, bytes_accessed=8 * (R + C) * D, transcendentals=5 * R * C),
    )(noise, data)


def per_device(Z, Y, noise, data, times):
    targets = targets_of(Z, Y, noise, data)
    path = (1.0 - times)[:, None] * noise + times[:, None] * targets
    return (path, targets - noise)


def solution(mesh):
    Z, Y = mesh.shape["row"], mesh.shape["col"] // QUAD
    in_specs = (P(("row", "col"), None), P(("col", "row"), None), P(("row", "col")))
    out_specs = (P(("row", "col"), None), P(("row", "col"), None))
    return jax.shard_map(
        functools.partial(per_device, Z, Y), mesh=mesh, in_specs=in_specs, out_specs=out_specs,
        check_vma=False,
    )
```
